32 devices in a mesh: window: 2 (over x), tile: 8 (over z, y), member: 2 (over core).
Axes of the slice: x: 2, y: 2, z: 4, core: 2. Of those that a mesh axis runs over, the one named last changes fastest.
Arguments:
- control: float32 [40, 192, 2048], P(('window', 'member'), 'tile'), parts along dimension 0, may hold values from -6 to 6
- velocity: float32 [40, 192, 2048], P(('window', 'member'), 'tile'), parts along dimension 0, may hold values from -6 to 6
- perturb: bfloat16 [40, 3, 192, 2048], P(('window', 'member'), None, 'tile'), parts along dimension 0, as said below
- adjoint_forcing: float32 [4, 3, 192, 2048], P(('window', 'member'), None, 'tile'), parts along dimension 0, as said below
- slot_owner: int32 [6, 8], P('window', 'tile'), parts along dimension 0, may hold values from 0 to 1
- taps_x: float32 [7], replicated, may hold values from 0.3 to 1
- taps_y: float32 [7], replicated, may hold values from 0.3 to 1
- vertical_mix: float32 [64, 64], replicated, may hold values from -0.75 to 0.75
Outputs:
- new_control: float32 [40, 192, 2048], P(('window', 'member'), 'tile'), parts along dimension 0
- new_velocity: float32 [40, 192, 2048], P(('window', 'member'), 'tile'), parts along dimension 0
The draws below stay inside these ranges and needn't reach their ends.
There are 2 independent parts, one for each index of `window`. The reference program is written for one: setup_inputs(seed, part) draws one part's arguments, and reference() takes and returns one part's arrays. A program takes and returns all parts, laid end to end along the dimension named above; an argument that names none is the same for every part. Nothing has to cross between parts.
Inputs may be any that keep to these rules, and one draw needn't show every extreme that they name: `adjoint_forcing`: gradient values of order one to some tens. `perturb`: perturbation values of order one.
All inputs are finite; a program needn't handle non-finite values.
Results may differ from the reference program's by a relative error of at most 0.0003.
Values sent between devices are 32-bit elements; how exact they have to be, the bound alone decides.
No kernel may reach another device: no remote copies, remote signals or barrier semaphores. Data moves between devices by JAX's collectives and lax.ppermute only.
A program may use at most 128 MiB of HBM per device.

```python
import jax
import jax.numpy as jnp
from jax import lax

NZ = 64
SLOTS = 3
TX = 24
NY = 32
MEMBERS = 20
GROUPS = 2
NTILES = 8
NX = 192
CELLS = 2048


def draw_perturb(key, part):
    key = jax.random.fold_in(key, 11)
    first, second = jax.random.split(key, 2)
    shape = (MEMBERS, SLOTS, NX, NY * NZ)
    common_shape = (MEMBERS, SLOTS, 1, NY * NZ)
    weight = 0.7071
    single = jax.random.truncated_normal(first, -4.0, 4.0, shape, jnp.float32)
    shared = jax.random.truncated_normal(second, -4.0, 4.0, common_shape, jnp.float32)
    values = jnp.clip(weight * single + weight * shared, -6.0, 6.0)
    return values.astype(jnp.bfloat16)


def draw_adjoint_forcing(key, part):
    key = jax.random.fold_in(key, 7)
    first = jax.random.fold_in(key, 0)
    third = jax.random.fold_in(key, 2)
    shape = (GROUPS, SLOTS, NX, NY * NZ)
    common_shape = (1, SLOTS, 1, NY * NZ)
    weight = 0.7071
    ramp = 1.0 + 2.0 * jnp.arange(NX, dtype=jnp.float32) / max(NX - 1, 1)
    ramp = ramp[None, None, :, None]
    base = jax.random.truncated_normal(first, -4.0, 4.0, shape, jnp.float32)
    shared = jax.random.truncated_normal(third, -4.0, 4.0, common_shape, jnp.float32)
    values = (weight * base + weight * shared) * ramp
    return values.astype(jnp.float32)


def set_ends(result, rng, smallest, high):
    longest = result.shape.index(max(result.shape))
    spots = []
    for shift in (0, 1):
        where = [jax.random.randint(jax.random.fold_in(rng, axis), (), 0, length) for axis, length in enumerate(result.shape)]
        where[longest] = (where[longest] + shift) % result.shape[longest]
        spots.append(tuple(where))
    return result.at[spots[0]].set(smallest).at[spots[1]].set(high)


def block_levels(own_key, shape, cuts, low, top_value):
    factor_of = 1.0
    for position, blocks in cuts:
        draws = jax.random.uniform(jax.random.fold_in(jax.random.fold_in(own_key, 6), position), (blocks,), jnp.float32, low / len(cuts), top_value / len(cuts))
        factor_of = factor_of * jnp.repeat(jnp.exp(draws), shape[position] // blocks).reshape((-1,) + (1,) * (len(shape) - 1 - position))
    return factor_of


def noise(rng, shape, scale, reach, shards=(), held_as=jnp.bfloat16):
    result = scale * jax.random.normal(rng, shape, jnp.float32)
    if shards:
        result = result * block_levels(rng, shape, shards, -0.22, 0.18)
    return jnp.clip(result, -reach, reach).astype(held_as)


def setup_inputs(seed: int = 0, part: int = 0) -> dict:
    arg_keys = jax.random.split(jax.random.key(seed), 9)
    own_keys = jax.random.split(jax.random.fold_in(arg_keys[8], part), 9)
    control = noise(own_keys[0], (MEMBERS, NX, CELLS), 1.0, 6.0, ((0, 2), (1, 8)), jnp.float32)
    velocity = noise(own_keys[1], (MEMBERS, NX, CELLS), 1.0, 6.0, ((0, 2), (1, 8)), jnp.float32)
    perturb = draw_perturb(jax.random.fold_in(jax.random.fold_in(arg_keys[8], part), 71), part)
    adjoint_forcing = draw_adjoint_forcing(jax.random.fold_in(jax.random.fold_in(arg_keys[8], part), 71), part)
    slot_owner = set_ends(jax.random.randint(own_keys[4], (SLOTS, NTILES), 0, GROUPS), jax.random.fold_in(own_keys[4], 1), 0, GROUPS - 1).astype(jnp.int32)
    taps_x = jnp.clip(jax.random.uniform(arg_keys[5], (7,), jnp.float32, 0.3, 1.0), 0.3, 1.0)
    taps_y = jnp.clip(jax.random.uniform(arg_keys[6], (7,), jnp.float32, 0.3, 1.0), 0.3, 1.0)
    vertical_mix = noise(arg_keys[7], (NZ, NZ), NZ ** -0.5, 0.75, (), jnp.float32)
    return dict(control=control, velocity=velocity, perturb=perturb, adjoint_forcing=adjoint_forcing, slot_owner=slot_owner, taps_x=taps_x, taps_y=taps_y, vertical_mix=vertical_mix)


def reference(control, velocity, perturb, adjoint_forcing, slot_owner, taps_x, taps_y, vertical_mix):
    tile_of_row = jnp.arange(NX) // TX
    selected = slot_owner[:, tile_of_row]
    forcing = jnp.zeros((SLOTS, NX, CELLS), jnp.float32)
    for group in range(GROUPS):
        forcing = jnp.where((selected == group)[:, :, None], adjoint_forcing[group], forcing)
    product = jnp.zeros((MEMBERS, NX, CELLS), jnp.float32)
    for slot in range(SLOTS):
        product = product + perturb[:, slot].astype(jnp.float32) * forcing[slot][None]
    padded = jnp.pad(product, ((0, 0), (3, 3), (0, 0)))
    along_x = jnp.zeros_like(product)
    for offset in range(7):
        along_x = along_x + taps_x[offset] * padded[:, offset:offset + NX]
    shaped = along_x.reshape(MEMBERS, NX, NY, NZ)
    padded_y = jnp.pad(shaped, ((0, 0), (0, 0), (3, 3), (0, 0)))
    along_y = jnp.zeros_like(shaped)
    for offset in range(7):
        along_y = along_y + taps_y[offset] * padded_y[:, :, offset:offset + NY]
    mixed = jnp.einsum('mxyw,wz->mxyz', along_y, vertical_mix, precision=lax.Precision.HIGHEST)
    gradient = control + mixed.reshape(MEMBERS, NX, CELLS)
    mean_square = jnp.sum(gradient * gradient) / (MEMBERS * NX * CELLS)
    scale = lax.rsqrt(mean_square + 1e-06)
    new_velocity = 0.9 * velocity + scale * gradient
    new_control = control - 0.5 * new_velocity
    return (new_control, new_velocity)
```

```python
import functools

import jax
import jax.numpy as jnp
from jax import lax
from jax.experimental import pallas as pl
from jax.experimental.pallas import tpu as pltpu
from jax.sharding import PartitionSpec as P

NZ = 64
SLOTS = 3
BLOCK = 256
BAND = 3 * BLOCK
F32 = jnp.float32
BF16 = jnp.bfloat16

VMEM = pl.BlockSpec(memory_space=pltpu.VMEM)
SMEM = pl.BlockSpec(memory_space=pltpu.SMEM)
ANY = pl.BlockSpec(memory_space=pl.ANY)


def params(mib):
    return pltpu.CompilerParams(vmem_limit_bytes=mib * 1024 * 1024)


def cost(flops, nbytes):
    return pl.CostEstimate(flops=flops, bytes_accessed=nbytes, transcendentals=0)


def pack(ref, member, rows):
    cells = rows.shape[1]
    if member < 8:
        ref[3 * member : 3 * member + 3, 0:cells] = rows
        return
    part = cells // 4
    for quarter in range(4):
        top = 6 * quarter + 3 * (member - 8)
        ref[top : top + 3, cells : cells + part] = rows[:, part * quarter : part * (quarter + 1)]


def unpack(ref, member, cells):
    if member < 8:
        return ref[3 * member : 3 * member + 3, 0:cells]
    part = cells // 4
    pieces = []
    for quarter in range(4):
        top = 6 * quarter + 3 * (member - 8)
        pieces.append(ref[top : top + 3, cells : cells + part])
    return jnp.concatenate(pieces, axis=1)


def split(value):
    high = value.astype(BF16)
    return high, (value - high.astype(F32)).astype(BF16)


def dot3(left, high, low):
    left_high, left_low = split(left)
    total = jnp.dot(left_high, low, preferred_element_type=F32)
    total += jnp.dot(left_low, high, preferred_element_type=F32)
    return total + jnp.dot(left_high, high, preferred_element_type=F32)


def build_band(mix, taps_ref, tap_of, high_ref, low_ref):
    wide = jnp.concatenate([mix] * (BLOCK // NZ), axis=1)
    group = lax.broadcasted_iota(jnp.int32, (1, BLOCK), 1) // NZ
    for a in range(BAND // NZ):
        factor = jnp.zeros((1, BLOCK), F32)
        for b in range(BLOCK // NZ):
            k = tap_of(a, b)
            if 0 <= k <= 6:
                factor = jnp.where(group == b, taps_ref[k], factor)
        high, low = split(wide * factor)
        high_ref[NZ * a : NZ * (a + 1), :] = high
        low_ref[NZ * a : NZ * (a + 1), :] = low


def border_kernel(owner_ref, perturb_ref, mine_ref, other_ref, up_ref, down_ref):
    members, _, rows, cells = perturb_ref.shape
    me = lax.axis_index("member")
    fields = []
    for slot in range(SLOTS):
        valid = owner_ref[slot, 0] == me
        pair = []
        for start in (0, rows - 8):
            here = mine_ref[0, slot, start : start + 8, :]
            there = other_ref[0, slot, start : start + 8, :]
            pair.append(jnp.where(valid, here, there))
        fields.append(pair)
    for member in range(members):
        for side, start in enumerate((0, rows - 8)):
            total = jnp.zeros((8, cells), F32)
            for slot in range(SLOTS):
                total += perturb_ref[member, slot, start : start + 8, :].astype(F32) * fields[slot][side]
            if side == 0:
                pack(down_ref, member, total[0:3])
            else:
                pack(up_ref, member, total[5:8])


def bulk_kernel(
    owner_ref, taps_x_ref, taps_y_ref, mix_ref, perturb_ref, mine_ref, other_ref, control_ref,
    local_ref, cross_up_ref, cross_down_ref, square_ref,
    field, filtered, turned, high, low, high_t, low_t,
):
    members, _, rows, cells = perturb_ref.shape
    tall = rows + 16
    me = lax.axis_index("member")
    tile = lax.axis_index("tile")
    tiles = lax.axis_size("tile")
    mix = mix_ref[...]
    build_band(mix, taps_y_ref, lambda a, b: a - b - 1, high, low)
    build_band(mix.T, taps_y_ref, lambda a, b: b - a + 7, high_t, low_t)
    for slot in range(SLOTS):
        field[slot] = jnp.where(owner_ref[slot, 0] == me, mine_ref[0, slot], other_ref[0, slot])
    filtered[:, :, 0:BLOCK] = jnp.zeros((members, tall, BLOCK), F32)
    filtered[:, :, BLOCK + cells :] = jnp.zeros((members, tall, BLOCK), F32)
    turned[:, 0:BLOCK] = jnp.zeros((members * 16, BLOCK), F32)
    turned[:, BLOCK + cells :] = jnp.zeros((members * 16, BLOCK), F32)
    part = 512

    def rows_step(member, carry):
        for start in range(0, cells, part):
            lanes = slice(start, start + part)
            product = jnp.zeros((rows, part), F32)
            for slot in range(SLOTS):
                product += perturb_ref[member, slot, :, lanes].astype(F32) * field[slot, :, lanes]
            edge = jnp.zeros((16, part), F32)
            padded = jnp.concatenate([edge, product, edge], axis=0)
            total = taps_x_ref[0] * padded[5 : 5 + tall]
            for k in range(1, 7):
                total += taps_x_ref[k] * padded[5 + k : 5 + k + tall]
            filtered[member, :, BLOCK + start : BLOCK + start + part] = total
        return carry

    lax.fori_loop(0, members, rows_step, 0)
    weight_top = jnp.where(tile > 0, 1.0, 0.0).astype(F32)
    weight_bottom = jnp.where(tile < tiles - 1, 1.0, 0.0).astype(F32)

    def block_step(j, carry):
        lanes = pl.ds(pl.multiple_of(j * BLOCK, BLOCK), BAND)
        out = pl.ds(pl.multiple_of(j * BLOCK, BLOCK), BLOCK)
        left = filtered[:, :, lanes].reshape(members * tall, BAND)
        result = dot3(left, high[...], low[...]).reshape(members, tall, BLOCK)
        local = control_ref[:, :, out] + result[:, 8 : 8 + rows]
        local_ref[:, :, out] = local
        total = jnp.sum((local * local).reshape(members * rows // 8, 8, BLOCK), axis=0)
        above, below = result[:, 0:8], result[:, 8 + rows :]
        total += weight_top * jnp.sum(above * above, axis=0)
        total += weight_bottom * jnp.sum(below * below, axis=0)
        return carry + total[:, 0:128] + total[:, 128:256]

    square_ref[...] = lax.fori_loop(0, cells // BLOCK, block_step, jnp.zeros((8, 128), F32))

    def turn_step(member, carry):
        for start in range(0, cells, part):
            lanes = slice(start, start + part)
            zero = jnp.zeros((8, part), F32)
            top = jnp.concatenate([zero, local_ref[member, 0:8, lanes]], axis=0)
            bottom = jnp.concatenate([local_ref[member, rows - 8 : rows, lanes], zero], axis=0)
            first = taps_x_ref[0] * top[8:16] + taps_x_ref[1] * top[7:15] + taps_x_ref[2] * top[6:14]
            last = taps_x_ref[6] * bottom[0:8] + taps_x_ref[5] * bottom[1:9] + taps_x_ref[4] * bottom[2:10]
            both = jnp.concatenate([first, last], axis=0)
            turned[pl.ds(pl.multiple_of(member * 16, 16), 16), BLOCK + start : BLOCK + start + part] = both
        return carry

    lax.fori_loop(0, members, turn_step, 0)
    adjoint = filtered

    def turn_block(j, carry):
        lanes = pl.ds(pl.multiple_of(j * BLOCK, BLOCK), BAND)
        out = pl.ds(pl.multiple_of(j * BLOCK, BLOCK), BLOCK)
        result = dot3(turned[:, lanes], high_t[...], low_t[...])
        adjoint[:, 0:16, out] = result.reshape(members, 16, BLOCK)
        return carry

    lax.fori_loop(0, cells // BLOCK, turn_block, 0)
    for member in range(members):
        pack(cross_up_ref, member, adjoint[member, 0:3, 0:cells])
        pack(cross_down_ref, member, adjoint[member, 13:16, 0:cells])


def cross_kernel(square_ref, cross_up_ref, cross_down_ref, from_left_ref, from_right_ref, total_ref):
    rows, width = cross_up_ref.shape
    total = jnp.zeros((8, 128), F32)
    part = 512
    for row in range(0, rows, 8):
        for start in range(0, width, part):
            lanes = slice(start, start + part)
            value = cross_up_ref[row : row + 8, lanes] * from_left_ref[row : row + 8, lanes]
            value += cross_down_ref[row : row + 8, lanes] * from_right_ref[row : row + 8, lanes]
            for lane in range(0, part, 128):
                total += value[:, lane : lane + 128]
    total_ref[...] = square_ref[...] + 2.0 * total


def correct_kernel(
    taps_x_ref, taps_y_ref, mix_ref, from_left_ref, from_right_ref, correction_ref, filtered, high, low
):
    members, _, cells = correction_ref.shape
    build_band(mix_ref[...], taps_y_ref, lambda a, b: a - b - 1, high, low)
    filtered[:, :, 0:BLOCK] = jnp.zeros((members, 16, BLOCK), F32)
    filtered[:, :, BLOCK + cells :] = jnp.zeros((members, 16, BLOCK), F32)
    for member in range(members):
        left = unpack(from_left_ref, member, cells)
        right = unpack(from_right_ref, member, cells)
        first = jnp.concatenate([left, jnp.zeros((13, cells), F32)], axis=0)
        last = jnp.concatenate([jnp.zeros((13, cells), F32), right], axis=0)
        top = taps_x_ref[0] * first[0:8] + taps_x_ref[1] * first[1:9] + taps_x_ref[2] * first[2:10]
        bottom = taps_x_ref[6] * last[8:16] + taps_x_ref[5] * last[7:15] + taps_x_ref[4] * last[6:14]
        filtered[member, 0:8, BLOCK : BLOCK + cells] = top
        filtered[member, 8:16, BLOCK : BLOCK + cells] = bottom

    def block_step(j, carry):
        lanes = pl.ds(pl.multiple_of(j * BLOCK, BLOCK), BAND)
        out = pl.ds(pl.multiple_of(j * BLOCK, BLOCK), BLOCK)
        left = filtered[:, :, lanes].reshape(members * 16, BAND)
        correction_ref[:, :, out] = dot3(left, high[...], low[...]).reshape(members, 16, BLOCK)
        return carry

    lax.fori_loop(0, cells // BLOCK, block_step, 0)


def update_kernel(
    entries, near_ref, far_ref, control_ref, velocity_ref, local_ref, correction_ref,
    new_control_hbm, new_velocity_hbm, new_control, new_velocity, sems,
):
    members, rows, cells = control_ref.shape
    mean = jnp.sum(near_ref[...] + far_ref[...], keepdims=True) / entries
    scale = lax.rsqrt(mean + 1e-06)
    copies = []
    for member in range(members):
        for start in range(0, rows, 8):
            tile = slice(start, start + 8)
            gradient = local_ref[member, tile]
            if start == 0:
                gradient += correction_ref[member, 0:8]
            if start == rows - 8:
                gradient += correction_ref[member, 8:16]
            moved = 0.9 * velocity_ref[member, tile] + scale * gradient
            new_velocity[member, tile] = moved
            new_control[member, tile] = control_ref[member, tile] - 0.5 * moved
        for which, (src, dst) in enumerate(((new_control, new_control_hbm), (new_velocity, new_velocity_hbm))):
            copy = pltpu.make_async_copy(src.at[member], dst.at[member], sems.at[which, member])
            copy.start()
            copies.append(copy)
    for copy in copies:
        copy.wait()


def body(control, velocity, perturb, adjoint_forcing, slot_owner, taps_x, taps_y, vertical_mix):
    members, rows, cells = control.shape
    tiles = lax.axis_size("tile")
    groups = lax.axis_size("member")
    swap = [(0, 1), (1, 0)]
    other = lax.ppermute(adjoint_forcing, "member", swap)
    packed = jax.ShapeDtypeStruct((24, cells + cells // 4), F32)
    up, down = pl.pallas_call(
        border_kernel,
        name="border_product",
        out_shape=(packed, packed),
        in_specs=[SMEM, VMEM, VMEM, VMEM],
        out_specs=(VMEM, VMEM),
        compiler_params=params(16),
        cost_estimate=cost(4_000_000, 4_000_000),
    )(slot_owner, perturb, adjoint_forcing, other)
    from_left = lax.ppermute(up, "tile", [(i, i + 1) for i in range(tiles - 1)])
    from_right = lax.ppermute(down, "tile", [(i + 1, i) for i in range(tiles - 1)])
    wide = cells + 2 * BLOCK
    band = pltpu.VMEM((BAND, BLOCK), BF16)
    local, cross_up, cross_down, square = pl.pallas_call(
        bulk_kernel,
        name="bulk",
        out_shape=(
            jax.ShapeDtypeStruct(control.shape, F32), packed, packed, jax.ShapeDtypeStruct((8, 128), F32),
        ),
        in_specs=[SMEM, SMEM, SMEM, VMEM, VMEM, VMEM, VMEM, VMEM],
        out_specs=(VMEM, VMEM, VMEM, VMEM),
        scratch_shapes=[
            pltpu.VMEM((SLOTS, rows, cells), F32),
            pltpu.VMEM((members, rows + 16, wide), F32),
            pltpu.VMEM((members * 16, wide), F32),
            band, band, band, band,
        ],
        compiler_params=params(32),
        cost_estimate=cost(9_000_000_000, 12_000_000),
    )(slot_owner, taps_x, taps_y, vertical_mix, perturb, adjoint_forcing, other, control)
    near = pl.pallas_call(
        cross_kernel,
        name="cross_term",
        out_shape=jax.ShapeDtypeStruct((8, 128), F32),
        in_specs=[VMEM] * 5,
        out_specs=VMEM,
        compiler_params=params(8),
        cost_estimate=cost(200_000, 1_000_000),
    )(square, cross_up, cross_down, from_left, from_right)
    correction = pl.pallas_call(
        correct_kernel,
        name="border_correction",
        out_shape=jax.ShapeDtypeStruct((members, 16, cells), F32),
        in_specs=[SMEM, SMEM, VMEM, VMEM, VMEM],
        out_specs=VMEM,
        scratch_shapes=[pltpu.VMEM((members, 16, wide), F32), band, band],
        compiler_params=params(16),
        cost_estimate=cost(2_000_000_000, 2_000_000),
    )(taps_x, taps_y, vertical_mix, from_left, from_right)
    steps = [("member", swap)]
    width = 1
    while width < tiles:
        steps.append(("tile", [(i, i ^ width) for i in range(tiles)]))
        width *= 2
    for axis, pairs in steps[:-1]:
        near = near + lax.ppermute(near, axis, pairs)
    far = lax.ppermute(near, *steps[-1])
    entries = members * groups * rows * tiles * cells
    whole = jax.ShapeDtypeStruct(control.shape, F32)
    return tuple(
        pl.pallas_call(
            functools.partial(update_kernel, float(entries)),
            name="update",
            out_shape=(whole, whole),
            in_specs=[VMEM] * 6,
            out_specs=(ANY, ANY),
            scratch_shapes=[
                pltpu.VMEM(control.shape, F32),
                pltpu.VMEM(control.shape, F32),
                pltpu.SemaphoreType.DMA((2, members)),
            ],
            compiler_params=params(16),
            cost_estimate=cost(3_000_000, 12_000_000),
        )(near, far, control, velocity, local, correction)
    )


def solution(mesh):
    placed = (
        P(("window", "member"), "tile", None),
        P(("window", "member"), "tile", None),
        P(("window", "member"), None, "tile", None),
        P(("window", "member"), None, "tile", None),
        P("window", "tile"),
        P(),
        P(),
        P(),
    )
    return jax.shard_map(
        body,
        mesh=mesh,
        in_specs=placed,
        out_specs=(P(("window", "member"), "tile", None), P(("window", "member"), "tile", None)),
        check_vma=False,
    )
```

```python
import functools

import jax
import jax.numpy as jnp
from jax import lax
from jax.experimental import pallas as pl
from jax.experimental.pallas import tpu as pltpu
from jax.sharding import PartitionSpec as P

NZ = 64
SLOTS = 3
LANES = 128
EDGE = 3
F32 = jnp.float32
BF16 = jnp.bfloat16

VMEM = pl.BlockSpec(memory_space=pltpu.VMEM)
SMEM = pl.BlockSpec(memory_space=pltpu.SMEM)
HBM = pl.BlockSpec(memory_space=pltpu.HBM)


def params(mib):
    return pltpu.CompilerParams(vmem_limit_bytes=mib * 1024 * 1024)


def cost(flops, nbytes):
    return pl.CostEstimate(flops=flops, bytes_accessed=nbytes, transcendentals=0)


def in_hbm(array):
    return pltpu.with_memory_space_constraint(array, pltpu.HBM)


def split(value):
    high = value.astype(BF16)
    return high, (value - high.astype(F32)).astype(BF16)


def build_mix(mix, out_ref):
    zero = jnp.zeros((NZ, NZ), F32)
    pair = jnp.concatenate(
        [jnp.concatenate([mix, zero], axis=1), jnp.concatenate([zero, mix], axis=1)], axis=0
    )
    high, low = split(pair)
    out_ref[0:LANES, 0:LANES] = high
    out_ref[LANES:, 0:LANES] = high
    out_ref[0:LANES, LANES:] = low
    out_ref[LANES:, LANES:] = jnp.zeros((LANES, LANES), BF16)


def columns(tiles, taps):
    count = len(tiles)
    lower = lax.broadcasted_iota(jnp.int32, tiles[0].shape, 1) < NZ
    zero = jnp.zeros_like(tiles[0])
    turned = [pltpu.roll(tile, NZ, 1) for tile in tiles]
    between = {}
    for t in range(-1, count):
        first = turned[t] if t >= 0 else zero
        second = turned[t + 1] if t + 1 < count else zero
        between[t] = jnp.where(lower, first, second)
    outs = []
    for t in range(count):
        total = taps[3] * tiles[t]
        for k, at in ((1, t - 1), (5, t + 1)):
            if 0 <= at < count:
                total += taps[k] * tiles[at]
        for k, at in ((0, t - 2), (2, t - 1), (4, t), (6, t + 1)):
            if at in between:
                total += taps[k] * between[at]
        outs.append(total)
    return outs


def store_split(ref, stride, row, upper, lower):
    for t, (first, second) in enumerate(zip(upper, lower)):
        high, low = split(jnp.concatenate([first, second], axis=0))
        ref[stride * t + row : stride * t + row + 16, 0:LANES] = high
        ref[stride * t + row : stride * t + row + 16, LANES:] = low


def mixed(ref, start, size, matrix):
    both = jnp.dot(ref[start : start + size, :], matrix, preferred_element_type=F32)
    return both[:, 0:LANES] + both[:, LANES:]


def lanes_of(t):
    return slice(LANES * t, LANES * (t + 1))


def stage_kernel(perturb_hbm, mine_hbm, perturb_ref, mine_ref, sems):
    members = perturb_ref.shape[0]
    copies = [pltpu.make_async_copy(mine_hbm, mine_ref, sems.at[members])]
    for member in range(members):
        copies.append(pltpu.make_async_copy(perturb_hbm.at[member], perturb_ref.at[member], sems.at[member]))
    for copy in copies:
        copy.start()
    for copy in copies:
        copy.wait()


def border_kernel(owner_ref, perturb_ref, mine_ref, other_ref, up_ref, down_ref):
    members, _, rows, cells = perturb_ref.shape
    me = lax.axis_index("member")
    valid = [owner_ref[slot] == me for slot in range(SLOTS)]
    for t in range(cells // LANES):
        for start, ref, first in ((0, down_ref, 0), (rows - 8, up_ref, 8 - EDGE)):
            fields = [
                jnp.where(
                    valid[slot],
                    mine_ref[0, slot, start : start + 8, lanes_of(t)],
                    other_ref[0, slot, start : start + 8, lanes_of(t)],
                )
                for slot in range(SLOTS)
            ]
            for member in range(members):
                total = perturb_ref[member, 0, start : start + 8, lanes_of(t)].astype(F32) * fields[0]
                for slot in range(1, SLOTS):
                    total += perturb_ref[member, slot, start : start + 8, lanes_of(t)].astype(F32) * fields[slot]
                at = EDGE * (members * t + member)
                ref[at : at + EDGE, :] = total[first : first + EDGE]


def bulk_kernel(
    owner_ref, taps_x_ref, taps_y_ref, mix_ref, perturb_ref, mine_ref, other_ref, control_hbm, velocity_hbm,
    local_ref, cross_up_ref, cross_down_ref, square_ref, control_ref, velocity_ref,
    field, rows_of, left, turned, matrix, matrix_t, sems,
):
    members, _, rows, cells = perturb_ref.shape
    count = cells // LANES
    tall = rows + 16
    control_copy = pltpu.make_async_copy(control_hbm, control_ref, sems.at[0])
    velocity_copy = pltpu.make_async_copy(velocity_hbm, velocity_ref, sems.at[1])
    control_copy.start()
    velocity_copy.start()
    me = lax.axis_index("member")
    tile = lax.axis_index("tile")
    tiles = lax.axis_size("tile")
    taps_x = [taps_x_ref[k] for k in range(7)]
    taps_y = [taps_y_ref[k] for k in range(7)]
    build_mix(mix_ref[...], matrix)
    build_mix(mix_ref[...].T, matrix_t)
    for slot in range(SLOTS):
        field[slot] = jnp.where(owner_ref[slot] == me, mine_ref[0, slot], other_ref[0, slot])
    for half in range(2):
        rows_of[half, :, 0:8, :] = jnp.zeros((count, 8, LANES), F32)
        rows_of[half, :, tall - 8 : tall, :] = jnp.zeros((count, 8, LANES), F32)
    weight_top = jnp.where(tile > 0, 1.0, 0.0).astype(F32)
    weight_bottom = jnp.where(tile < tiles - 1, 1.0, 0.0).astype(F32)

    def pair_step(pair, carry):
        for half in range(2):
            member = 2 * pair + half
            for t in range(count):
                product = perturb_ref[member, 0, :, lanes_of(t)].astype(F32) * field[0, :, lanes_of(t)]
                for slot in range(1, SLOTS):
                    product += perturb_ref[member, slot, :, lanes_of(t)].astype(F32) * field[slot, :, lanes_of(t)]
                rows_of[half, t, 8 : 8 + rows, :] = product
        blocks = []
        for half in range(2):
            for row in range(0, tall, 8):
                used = range(7)
                if row == 0:
                    used = range(4, 7)
                if row == tall - 8:
                    used = range(0, 3)
                block = []
                for t in range(count):
                    total = None
                    for k in used:
                        term = taps_x[k] * rows_of[half, t, row + k - 3 : row + k + 5, :]
                        total = term if total is None else total + term
                    block.append(total)
                blocks.append(columns(block, taps_y))
                if len(blocks) == 2:
                    at = half * tall + row - 8
                    store_split(left, 2 * tall, at, *blocks)
                    blocks = []
        pl.when(pair == 0)(control_copy.wait)
        group = 4
        for first in range(0, count, group):
            size = 2 * tall
            out = mixed(left, size * first, size * group, matrix[...])
            for t in range(first, first + group):
                for half in range(2):
                    member = 2 * pair + half
                    base = size * (t - first) + tall * half
                    here = control_ref[member, :, lanes_of(t)] + out[base + 8 : base + 8 + rows]
                    local_ref[member, :, lanes_of(t)] = here
                    squared = here * here
                    for row in range(0, rows, 8):
                        carry += squared[row : row + 8]
                    above, below = out[base : base + 8], out[base + tall - 8 : base + tall]
                    carry += weight_top * (above * above) + weight_bottom * (below * below)
        return carry

    square_ref[...] = lax.fori_loop(0, members // 2, pair_step, jnp.zeros((8, LANES), F32))
    velocity_copy.wait()
    back = taps_y[::-1]

    def turn_step(pair, carry):
        for half in range(2):
            member = 2 * pair + half
            for t in range(count):
                rows_of[half, t, 8:16, :] = local_ref[member, 0:8, lanes_of(t)]
                rows_of[half, t, rows : rows + 8, :] = local_ref[member, rows - 8 : rows, lanes_of(t)]
        for half in range(2):
            first, last = [], []
            for t in range(count):
                total = taps_x[0] * rows_of[half, t, 8:16, :]
                other = taps_x[6] * rows_of[half, t, rows : rows + 8, :]
                for d in range(1, EDGE):
                    total += taps_x[d] * rows_of[half, t, 8 - d : 16 - d, :]
                    other += taps_x[6 - d] * rows_of[half, t, rows + d : rows + 8 + d, :]
                first.append(total)
                last.append(other)
            store_split(left, 32, 16 * half, columns(first, back), columns(last, back))
        out = mixed(left, 0, 32 * count, matrix_t[...])
        for t in range(count):
            for half in range(2):
                turned[2 * pair + half, t] = out[32 * t + 16 * half : 32 * t + 16 * half + 16]
        return carry

    lax.fori_loop(0, members // 2, turn_step, 0)
    for member in range(members):
        for t in range(count):
            at = EDGE * (members * t + member)
            cross_up_ref[at : at + EDGE, :] = turned[member, t, 0:EDGE, :]
            cross_down_ref[at : at + EDGE, :] = turned[member, t, 16 - EDGE : 16, :]


def cross_kernel(square_ref, cross_up_ref, cross_down_ref, from_left_ref, from_right_ref, total_ref):
    total = [jnp.zeros((8, LANES), F32) for _ in range(4)]
    for step, row in enumerate(range(0, cross_up_ref.shape[0], 8)):
        at = slice(row, row + 8)
        which = 2 * (step % 2)
        total[which] += cross_up_ref[at] * from_left_ref[at]
        total[which + 1] += cross_down_ref[at] * from_right_ref[at]
    total_ref[...] = square_ref[...] + 2.0 * ((total[0] + total[1]) + (total[2] + total[3]))


def correct_kernel(
    taps_x_ref, taps_y_ref, mix_ref, from_left_ref, from_right_ref, correction_ref, rows_of, left, matrix
):
    members, _, cells = correction_ref.shape
    count = cells // LANES
    taps_x = [taps_x_ref[k] for k in range(7)]
    taps_y = [taps_y_ref[k] for k in range(7)]
    build_mix(mix_ref[...], matrix)
    zero = jnp.zeros((8, LANES), F32)
    for member in range(members):
        for t in range(count):
            at = EDGE * (members * t + member)
            for row in range(0, 32, 8):
                rows_of[member, t, row : row + 8, :] = zero
            rows_of[member, t, 0:EDGE, :] = from_left_ref[at : at + EDGE, :]
            rows_of[member, t, 32 - EDGE : 32, :] = from_right_ref[at : at + EDGE, :]

    def pair_step(pair, carry):
        for half in range(2):
            member = 2 * pair + half
            first, last = [], []
            for t in range(count):
                total = taps_x[0] * rows_of[member, t, 0:8, :]
                other = taps_x[6] * rows_of[member, t, 24:32, :]
                for d in range(1, EDGE):
                    total += taps_x[d] * rows_of[member, t, d : 8 + d, :]
                    other += taps_x[6 - d] * rows_of[member, t, 24 - d : 32 - d, :]
                first.append(total)
                last.append(other)
            store_split(left, 32, 16 * half, columns(first, taps_y), columns(last, taps_y))
        out = mixed(left, 0, 32 * count, matrix[...])
        for t in range(count):
            for half in range(2):
                correction_ref[2 * pair + half, :, lanes_of(t)] = out[32 * t + 16 * half : 32 * t + 16 * half + 16]
        return carry

    lax.fori_loop(0, members // 2, pair_step, 0)


def update_kernel(
    entries, near_ref, far_ref, control_ref, velocity_ref, local_ref, correction_ref,
    new_control_hbm, new_velocity_hbm, new_control, new_velocity, sems,
):
    members, rows, cells = control_ref.shape
    mean = jnp.sum(near_ref[...] + far_ref[...], keepdims=True) / entries
    scale = lax.rsqrt(mean + 1e-06)
    copies = []
    for member in range(members):
        for start in range(0, rows, 8):
            tile = slice(start, start + 8)
            gradient = local_ref[member, tile]
            if start == 0:
                gradient += correction_ref[member, 0:8]
            if start == rows - 8:
                gradient += correction_ref[member, 8:16]
            moved = 0.9 * velocity_ref[member, tile] + scale * gradient
            new_velocity[member, tile] = moved
            new_control[member, tile] = control_ref[member, tile] - 0.5 * moved
        for which, (src, dst) in enumerate(((new_control, new_control_hbm), (new_velocity, new_velocity_hbm))):
            copy = pltpu.make_async_copy(src.at[member], dst.at[member], sems.at[which, member])
            copy.start()
            copies.append(copy)
    for copy in copies:
        copy.wait()


def body(control, velocity, perturb, adjoint_forcing, slot_owner, taps_x, taps_y, vertical_mix):
    members, rows, cells = control.shape
    count = cells // LANES
    tiles = lax.axis_size("tile")
    groups = lax.axis_size("member")
    owner = slot_owner.reshape(SLOTS)
    swap = [(0, 1), (1, 0)]
    other = lax.ppermute(adjoint_forcing, "member", swap)
    perturb, mine = pl.pallas_call(
        stage_kernel,
        name="stage",
        out_shape=(
            jax.ShapeDtypeStruct(perturb.shape, perturb.dtype),
            jax.ShapeDtypeStruct(adjoint_forcing.shape, F32),
        ),
        in_specs=[HBM, HBM],
        out_specs=(VMEM, VMEM),
        scratch_shapes=[pltpu.SemaphoreType.DMA((members + 1,))],
        compiler_params=params(8),
        cost_estimate=cost(0, 8_000_000),
    )(in_hbm(perturb), in_hbm(adjoint_forcing))
    packed = jax.ShapeDtypeStruct((EDGE * members * count, LANES), F32)
    up, down = pl.pallas_call(
        border_kernel,
        name="border_product",
        out_shape=(packed, packed),
        in_specs=[SMEM, VMEM, VMEM, VMEM],
        out_specs=(VMEM, VMEM),
        compiler_params=params(8),
        cost_estimate=cost(4_000_000, 4_000_000),
    )(owner, perturb, mine, other)
    from_left = lax.ppermute(up, "tile", [(i, i + 1) for i in range(tiles - 1)])
    from_right = lax.ppermute(down, "tile", [(i + 1, i) for i in range(tiles - 1)])
    matrix = pltpu.VMEM((2 * LANES, 2 * LANES), BF16)
    whole = jax.ShapeDtypeStruct(control.shape, F32)
    local, cross_up, cross_down, square, control, velocity = pl.pallas_call(
        bulk_kernel,
        name="bulk",
        out_shape=(whole, packed, packed, jax.ShapeDtypeStruct((8, LANES), F32), whole, whole),
        in_specs=[SMEM, SMEM, SMEM, VMEM, VMEM, VMEM, VMEM, HBM, HBM],
        out_specs=(VMEM,) * 6,
        scratch_shapes=[
            pltpu.VMEM((SLOTS, rows, cells), F32),
            pltpu.VMEM((2, count, rows + 16, LANES), F32),
            pltpu.VMEM((count * 2 * (rows + 16), 2 * LANES), BF16),
            pltpu.VMEM((members, count, 16, LANES), F32),
            matrix, matrix,
            pltpu.SemaphoreType.DMA((2,)),
        ],
        compiler_params=params(24),
        cost_estimate=cost(9_000_000_000, 12_000_000),
    )(owner, taps_x, taps_y, vertical_mix, perturb, mine, other, in_hbm(control), in_hbm(velocity))
    near = pl.pallas_call(
        cross_kernel,
        name="cross_term",
        out_shape=jax.ShapeDtypeStruct((8, LANES), F32),
        in_specs=[VMEM] * 5,
        out_specs=VMEM,
        compiler_params=params(8),
        cost_estimate=cost(200_000, 1_000_000),
    )(square, cross_up, cross_down, from_left, from_right)
    correction = pl.pallas_call(
        correct_kernel,
        name="border_correction",
        out_shape=jax.ShapeDtypeStruct((members, 16, cells), F32),
        in_specs=[SMEM, SMEM, VMEM, VMEM, VMEM],
        out_specs=VMEM,
        scratch_shapes=[
            pltpu.VMEM((members, count, 32, LANES), F32),
            pltpu.VMEM((count * 32, 2 * LANES), BF16),
            matrix,
        ],
        compiler_params=params(16),
        cost_estimate=cost(2_000_000_000, 2_000_000),
    )(taps_x, taps_y, vertical_mix, from_left, from_right)
    steps = [("member", swap)]
    width = 1
    while width < tiles:
        steps.append(("tile", [(i, i ^ width) for i in range(tiles)]))
        width *= 2
    for axis, pairs in steps[:-1]:
        near = near + lax.ppermute(near, axis, pairs)
    far = lax.ppermute(near, *steps[-1])
    entries = members * groups * rows * tiles * cells
    return tuple(
        pl.pallas_call(
            functools.partial(update_kernel, float(entries)),
            name="update",
            out_shape=(whole, whole),
            in_specs=[VMEM] * 6,
            out_specs=(HBM, HBM),
            scratch_shapes=[
                pltpu.VMEM(control.shape, F32),
                pltpu.VMEM(control.shape, F32),
                pltpu.SemaphoreType.DMA((2, members)),
            ],
            compiler_params=params(16),
            cost_estimate=cost(3_000_000, 12_000_000),
        )(near, far, control, velocity, local, correction)
    )


def solution(mesh):
    placed = (
        P(("window", "member"), "tile", None),
        P(("window", "member"), "tile", None),
        P(("window", "member"), None, "tile", None),
        P(("window", "member"), None, "tile", None),
        P("window", "tile"),
        P(),
        P(),
        P(),
    )
    return jax.shard_map(
        body,
        mesh=mesh,
        in_specs=placed,
        out_specs=(P(("window", "member"), "tile", None), P(("window", "member"), "tile", None)),
        check_vma=False,
    )
```

```python
import functools

import jax
import jax.numpy as jnp
from jax import lax
from jax.experimental import pallas as pl
from jax.experimental.pallas import tpu as pltpu
from jax.sharding import PartitionSpec as P

NZ = 64
SLOTS = 3
LANES = 128
EDGE = 3
F32 = jnp.float32
BF16 = jnp.bfloat16

VMEM = pl.BlockSpec(memory_space=pltpu.VMEM)
SMEM = pl.BlockSpec(memory_space=pltpu.SMEM)
HBM = pl.BlockSpec(memory_space=pltpu.HBM)


def params(mib):
    return pltpu.CompilerParams(vmem_limit_bytes=mib * 1024 * 1024)


def cost(flops, nbytes):
    return pl.CostEstimate(flops=flops, bytes_accessed=nbytes, transcendentals=0)


def in_hbm(array):
    return pltpu.with_memory_space_constraint(array, pltpu.HBM)


def split(value):
    high = value.astype(BF16)
    return high, (value - high.astype(F32)).astype(BF16)


def build_mix(mix, out_ref):
    zero = jnp.zeros((NZ, NZ), F32)
    pair = jnp.concatenate(
        [jnp.concatenate([mix, zero], axis=1), jnp.concatenate([zero, mix], axis=1)], axis=0
    )
    high, low = split(pair)
    out_ref[0:LANES, 0:LANES] = high
    out_ref[LANES:, 0:LANES] = high
    out_ref[0:LANES, LANES:] = low
    out_ref[LANES:, LANES:] = jnp.zeros((LANES, LANES), BF16)


def columns(tiles, taps):
    count = len(tiles)
    lower = lax.broadcasted_iota(jnp.int32, tiles[0].shape, 1) < NZ
    zero = jnp.zeros_like(tiles[0])
    turned = [pltpu.roll(tile, NZ, 1) for tile in tiles]
    between = {}
    for t in range(-1, count):
        first = turned[t] if t >= 0 else zero
        second = turned[t + 1] if t + 1 < count else zero
        between[t] = jnp.where(lower, first, second)
    outs = []
    for t in range(count):
        total = taps[3] * tiles[t]
        for k, at in ((1, t - 1), (5, t + 1)):
            if 0 <= at < count:
                total += taps[k] * tiles[at]
        for k, at in ((0, t - 2), (2, t - 1), (4, t), (6, t + 1)):
            if at in between:
                total += taps[k] * between[at]
        outs.append(total)
    return outs


def store_split(ref, stride, row, upper, lower):
    for t, (first, second) in enumerate(zip(upper, lower)):
        high, low = split(jnp.concatenate([first, second], axis=0))
        ref[stride * t + row : stride * t + row + 16, 0:LANES] = high
        ref[stride * t + row : stride * t + row + 16, LANES:] = low


def mixed(ref, start, size, matrix):
    both = jnp.dot(ref[start : start + size, :], matrix, preferred_element_type=F32)
    return both[:, 0:LANES] + both[:, LANES:]


def lanes_of(t):
    return slice(LANES * t, LANES * (t + 1))


def stage_kernel(perturb_hbm, mine_hbm, perturb_ref, mine_ref, border_ref, sems):
    members, _, rows, cells = perturb_ref.shape
    copies = []
    for member in range(members):
        copies.append(pltpu.make_async_copy(perturb_hbm.at[member], perturb_ref.at[member], sems.at[member]))
    copies.append(pltpu.make_async_copy(mine_hbm, mine_ref, sems.at[members]))
    for copy in copies:
        copy.start()
    for member in range(members):
        copies[member].wait()
        for slot in range(SLOTS):
            for t in range(cells // LANES):
                at = EDGE * (members * t + member)
                for side, start, first in ((0, 0, 0), (1, rows - 8, 8 - EDGE)):
                    value = perturb_ref[member, slot, start : start + 8, lanes_of(t)].astype(F32)
                    border_ref[slot, side, at : at + EDGE, :] = value[first : first + EDGE]
    copies[members].wait()


def border_kernel(owner_ref, border_ref, mine_ref, other_ref, up_ref, down_ref):
    _, _, rows, cells = mine_ref.shape
    total_rows = up_ref.shape[0]
    per_tile = total_rows // (cells // LANES)
    me = lax.axis_index("member")
    valid = [owner_ref[slot] == me for slot in range(SLOTS)]
    sublane = lax.broadcasted_iota(jnp.int32, (8, LANES), 0)
    phase = [lax.rem(sublane + shift, EDGE) for shift in range(EDGE)]
    is_zero = [value == 0 for value in phase]
    is_one = [value == 1 for value in phase]
    for start, ref, side in ((0, down_ref, 0), (rows - EDGE, up_ref, 1)):
        whole = {}
        for t in range(cells // LANES):
            for slot in range(SLOTS):
                lines = []
                for i in range(EDGE):
                    here = mine_ref[0, slot, start + i : start + i + 1, lanes_of(t)]
                    there = other_ref[0, slot, start + i : start + i + 1, lanes_of(t)]
                    lines.append(jnp.broadcast_to(jnp.where(valid[slot], here, there), (8, LANES)))
                for shift in range(EDGE):
                    whole[t, slot, shift] = jnp.where(
                        is_zero[shift], lines[0], jnp.where(is_one[shift], lines[1], lines[2])
                    )
            for row in range(0, total_rows, 8):
                if (row + 7) // per_tile != t:
                    continue
                total = None
                for slot in range(SLOTS):
                    field = whole[t, slot, row % EDGE]
                    if row // per_tile != t:
                        field = jnp.where(sublane < per_tile * t - row, whole[t - 1, slot, row % EDGE], field)
                    term = border_ref[slot, side, row : row + 8, :] * field
                    total = term if total is None else total + term
                ref[row : row + 8, :] = total


def bulk_kernel(
    owner_ref, taps_x_ref, taps_y_ref, mix_ref, perturb_ref, mine_ref, other_ref, control_hbm, velocity_hbm,
    local_ref, cross_up_ref, cross_down_ref, square_ref, control_ref, velocity_ref,
    field, rows_of, left, turned, matrix, matrix_t, sems,
):
    members, _, rows, cells = perturb_ref.shape
    count = cells // LANES
    tall = rows + 16
    control_copy = pltpu.make_async_copy(control_hbm, control_ref, sems.at[0])
    velocity_copy = pltpu.make_async_copy(velocity_hbm, velocity_ref, sems.at[1])
    control_copy.start()
    velocity_copy.start()
    me = lax.axis_index("member")
    tile = lax.axis_index("tile")
    tiles = lax.axis_size("tile")
    taps_x = [taps_x_ref[k] for k in range(7)]
    taps_y = [taps_y_ref[k] for k in range(7)]
    build_mix(mix_ref[...], matrix)
    build_mix(mix_ref[...].T, matrix_t)
    for slot in range(SLOTS):
        field[slot] = jnp.where(owner_ref[slot] == me, mine_ref[0, slot], other_ref[0, slot])
    for half in range(2):
        rows_of[half, :, 0:8, :] = jnp.zeros((count, 8, LANES), F32)
        rows_of[half, :, tall - 8 : tall, :] = jnp.zeros((count, 8, LANES), F32)
    weight_top = jnp.where(tile > 0, 1.0, 0.0).astype(F32)
    weight_bottom = jnp.where(tile < tiles - 1, 1.0, 0.0).astype(F32)

    def pair_step(pair, carry):
        for half in range(2):
            member = 2 * pair + half
            for t in range(count):
                product = perturb_ref[member, 0, :, lanes_of(t)].astype(F32) * field[0, :, lanes_of(t)]
                for slot in range(1, SLOTS):
                    product += perturb_ref[member, slot, :, lanes_of(t)].astype(F32) * field[slot, :, lanes_of(t)]
                rows_of[half, t, 8 : 8 + rows, :] = product
        blocks = []
        for half in range(2):
            for row in range(0, tall, 8):
                used = range(7)
                if row == 0:
                    used = range(4, 7)
                if row == tall - 8:
                    used = range(0, 3)
                block = []
                for t in range(count):
                    total = None
                    for k in used:
                        term = taps_x[k] * rows_of[half, t, row + k - 3 : row + k + 5, :]
                        total = term if total is None else total + term
                    block.append(total)
                blocks.append(columns(block, taps_y))
                if len(blocks) == 2:
                    at = half * tall + row - 8
                    store_split(left, 2 * tall, at, *blocks)
                    blocks = []
        pl.when(pair == 0)(control_copy.wait)
        group = 4
        for first in range(0, count, group):
            size = 2 * tall
            out = mixed(left, size * first, size * group, matrix[...])
            for t in range(first, first + group):
                for half in range(2):
                    member = 2 * pair + half
                    base = size * (t - first) + tall * half
                    here = control_ref[member, :, lanes_of(t)] + out[base + 8 : base + 8 + rows]
                    local_ref[member, :, lanes_of(t)] = here
                    squared = here * here
                    for row in range(0, rows, 8):
                        carry += squared[row : row + 8]
                    above, below = out[base : base + 8], out[base + tall - 8 : base + tall]
                    carry += weight_top * (above * above) + weight_bottom * (below * below)
        return carry

    square_ref[...] = lax.fori_loop(0, members // 2, pair_step, jnp.zeros((8, LANES), F32))
    velocity_copy.wait()
    back = taps_y[::-1]

    def turn_step(pair, carry):
        for half in range(2):
            member = 2 * pair + half
            for t in range(count):
                rows_of[half, t, 8:16, :] = local_ref[member, 0:8, lanes_of(t)]
                rows_of[half, t, rows : rows + 8, :] = local_ref[member, rows - 8 : rows, lanes_of(t)]
        for half in range(2):
            first, last = [], []
            for t in range(count):
                total = taps_x[0] * rows_of[half, t, 8:16, :]
                other = taps_x[6] * rows_of[half, t, rows : rows + 8, :]
                for d in range(1, EDGE):
                    total += taps_x[d] * rows_of[half, t, 8 - d : 16 - d, :]
                    other += taps_x[6 - d] * rows_of[half, t, rows + d : rows + 8 + d, :]
                first.append(total)
                last.append(other)
            store_split(left, 32, 16 * half, columns(first, back), columns(last, back))
        out = mixed(left, 0, 32 * count, matrix_t[...])
        for t in range(count):
            for half in range(2):
                turned[2 * pair + half, t] = out[32 * t + 16 * half : 32 * t + 16 * half + 16]
        return carry

    lax.fori_loop(0, members // 2, turn_step, 0)
    for member in range(members):
        for t in range(count):
            at = EDGE * (members * t + member)
            cross_up_ref[at : at + EDGE, :] = turned[member, t, 0:EDGE, :]
            cross_down_ref[at : at + EDGE, :] = turned[member, t, 16 - EDGE : 16, :]


def cross_kernel(square_ref, cross_up_ref, cross_down_ref, from_left_ref, from_right_ref, total_ref):
    total = [jnp.zeros((8, LANES), F32) for _ in range(4)]
    for step, row in enumerate(range(0, cross_up_ref.shape[0], 8)):
        at = slice(row, row + 8)
        which = 2 * (step % 2)
        total[which] += cross_up_ref[at] * from_left_ref[at]
        total[which + 1] += cross_down_ref[at] * from_right_ref[at]
    total_ref[...] = square_ref[...] + 2.0 * ((total[0] + total[1]) + (total[2] + total[3]))


def correct_kernel(
    taps_x_ref, taps_y_ref, mix_ref, from_left_ref, from_right_ref, local_ref, gradient_ref,
    rows_of, left, result, matrix,
):
    members, rows, cells = local_ref.shape
    count = cells // LANES
    here = EDGE * members
    taps_x = [taps_x_ref[k] for k in range(7)]
    taps_y = [taps_y_ref[k] for k in range(7)]
    build_mix(mix_ref[...], matrix)
    zero = jnp.zeros((8, LANES), F32)
    for t in range(count):
        rows_of[0, t, 24:32, :] = zero
        rows_of[0, t, 32:40, :] = zero
        rows_of[1, t, 0:8, :] = zero
        rows_of[1, t, 32:40, :] = zero
        rows_of[0, t, 0:here, :] = from_left_ref[here * t : here * (t + 1), :]
        rows_of[1, t, 8 : 8 + here, :] = from_right_ref[here * t : here * (t + 1), :]
    sublane = lax.broadcasted_iota(jnp.int32, (8, LANES), 0)
    blocks = []
    for side in range(2):
        for row in range(0, 32, 8):
            place = lax.rem(sublane + row, EDGE)
            if side == 0:
                factors = [jnp.where(place < EDGE - d, taps_x[d], 0.0) for d in range(EDGE)]
            else:
                factors = [jnp.where(place >= d, taps_x[6 - d], 0.0) for d in range(EDGE)]
            block = []
            for t in range(count):
                total = None
                for d in range(EDGE):
                    at = row + d if side == 0 else 8 + row - d
                    term = factors[d] * rows_of[side, t, at : at + 8, :]
                    total = term if total is None else total + term
                block.append(total)
            blocks.append(columns(block, taps_y))
            if len(blocks) == 2:
                store_split(left, 64, 32 * side + row - 8, *blocks)
                blocks = []
    group = 4
    for first in range(0, count, group):
        result[64 * first : 64 * (first + group), :] = mixed(left, 64 * first, 64 * group, matrix[...])
    for member in range(members):
        for t in range(count):
            at = 64 * t + EDGE * member
            gradient_ref[member, 0:EDGE, lanes_of(t)] += result[at : at + EDGE, :]
            gradient_ref[member, rows - EDGE : rows, lanes_of(t)] += result[at + 32 : at + 32 + EDGE, :]


def update_kernel(
    entries, near_ref, far_ref, control_ref, velocity_ref, gradient_ref,
    new_control_hbm, new_velocity_hbm, new_control, new_velocity, sems,
):
    members, rows, cells = control_ref.shape
    mean = jnp.sum(near_ref[...] + far_ref[...], keepdims=True) / entries
    scale = lax.rsqrt(mean + 1e-06)
    copies = []
    for member in range(members):
        for start in range(0, rows, 8):
            tile = slice(start, start + 8)
            moved = 0.9 * velocity_ref[member, tile] + scale * gradient_ref[member, tile]
            new_velocity[member, tile] = moved
            new_control[member, tile] = control_ref[member, tile] - 0.5 * moved
        for which, (src, dst) in enumerate(((new_control, new_control_hbm), (new_velocity, new_velocity_hbm))):
            copy = pltpu.make_async_copy(src.at[member], dst.at[member], sems.at[which, member])
            copy.start()
            copies.append(copy)
    for copy in copies:
        copy.wait()


def body(control, velocity, perturb, adjoint_forcing, slot_owner, taps_x, taps_y, vertical_mix):
    members, rows, cells = control.shape
    count = cells // LANES
    tiles = lax.axis_size("tile")
    groups = lax.axis_size("member")
    owner = slot_owner.reshape(SLOTS)
    swap = [(0, 1), (1, 0)]
    other = lax.ppermute(adjoint_forcing, "member", swap)
    edges = EDGE * members * count
    perturb, mine, border = pl.pallas_call(
        stage_kernel,
        name="stage",
        out_shape=(
            jax.ShapeDtypeStruct(perturb.shape, perturb.dtype),
            jax.ShapeDtypeStruct(adjoint_forcing.shape, F32),
            jax.ShapeDtypeStruct((SLOTS, 2, edges, LANES), F32),
        ),
        in_specs=[HBM, HBM],
        out_specs=(VMEM, VMEM, VMEM),
        scratch_shapes=[pltpu.SemaphoreType.DMA((members + 1,))],
        compiler_params=params(8),
        cost_estimate=cost(0, 8_000_000),
    )(in_hbm(perturb), in_hbm(adjoint_forcing))
    packed = jax.ShapeDtypeStruct((edges, LANES), F32)
    up, down = pl.pallas_call(
        border_kernel,
        name="border_product",
        out_shape=(packed, packed),
        in_specs=[SMEM, VMEM, VMEM, VMEM],
        out_specs=(VMEM, VMEM),
        compiler_params=params(8),
        cost_estimate=cost(4_000_000, 4_000_000),
    )(owner, border, mine, other)
    from_left = lax.ppermute(up, "tile", [(i, i + 1) for i in range(tiles - 1)])
    from_right = lax.ppermute(down, "tile", [(i + 1, i) for i in range(tiles - 1)])
    matrix = pltpu.VMEM((2 * LANES, 2 * LANES), BF16)
    whole = jax.ShapeDtypeStruct(control.shape, F32)
    local, cross_up, cross_down, square, control, velocity = pl.pallas_call(
        bulk_kernel,
        name="bulk",
        out_shape=(whole, packed, packed, jax.ShapeDtypeStruct((8, LANES), F32), whole, whole),
        in_specs=[SMEM, SMEM, SMEM, VMEM, VMEM, VMEM, VMEM, HBM, HBM],
        out_specs=(VMEM,) * 6,
        scratch_shapes=[
            pltpu.VMEM((SLOTS, rows, cells), F32),
            pltpu.VMEM((2, count, rows + 16, LANES), F32),
            pltpu.VMEM((count * 2 * (rows + 16), 2 * LANES), BF16),
            pltpu.VMEM((members, count, 16, LANES), F32),
            matrix, matrix,
            pltpu.SemaphoreType.DMA((2,)),
        ],
        compiler_params=params(24),
        cost_estimate=cost(9_000_000_000, 12_000_000),
    )(owner, taps_x, taps_y, vertical_mix, perturb, mine, other, in_hbm(control), in_hbm(velocity))
    near = pl.pallas_call(
        cross_kernel,
        name="cross_term",
        out_shape=jax.ShapeDtypeStruct((8, LANES), F32),
        in_specs=[VMEM] * 5,
        out_specs=VMEM,
        compiler_params=params(8),
        cost_estimate=cost(200_000, 1_000_000),
    )(square, cross_up, cross_down, from_left, from_right)
    gradient = pl.pallas_call(
        correct_kernel,
        name="border_correction",
        out_shape=whole,
        in_specs=[SMEM, SMEM, VMEM, VMEM, VMEM, VMEM],
        out_specs=VMEM,
        scratch_shapes=[
            pltpu.VMEM((2, count, 40, LANES), F32),
            pltpu.VMEM((count * 64, 2 * LANES), BF16),
            pltpu.VMEM((count * 64, LANES), F32),
            matrix,
        ],
        input_output_aliases={5: 0},
        compiler_params=params(16),
        cost_estimate=cost(2_000_000_000, 2_000_000),
    )(taps_x, taps_y, vertical_mix, from_left, from_right, local)
    steps = [("member", swap)]
    width = 1
    while width < tiles:
        steps.append(("tile", [(i, i ^ width) for i in range(tiles)]))
        width *= 2
    for axis, pairs in steps[:-1]:
        near = near + lax.ppermute(near, axis, pairs)
    far = lax.ppermute(near, *steps[-1])
    entries = members * groups * rows * tiles * cells
    return tuple(
        pl.pallas_call(
            functools.partial(update_kernel, float(entries)),
            name="update",
            out_shape=(whole, whole),
            in_specs=[VMEM] * 5,
            out_specs=(HBM, HBM),
            scratch_shapes=[
                pltpu.VMEM(control.shape, F32),
                pltpu.VMEM(control.shape, F32),
                pltpu.SemaphoreType.DMA((2, members)),
            ],
            compiler_params=params(16),
            cost_estimate=cost(3_000_000, 12_000_000),
        )(near, far, control, velocity, gradient)
    )


def solution(mesh):
    placed = (
        P(("window", "member"), "tile", None),
        P(("window", "member"), "tile", None),
        P(("window", "member"), None, "tile", None),
        P(("window", "member"), None, "tile", None),
        P("window", "tile"),
        P(),
        P(),
        P(),
    )
    return jax.shard_map(
        body,
        mesh=mesh,
        in_specs=placed,
        out_specs=(P(("window", "member"), "tile", None), P(("window", "member"), "tile", None)),
        check_vma=False,
    )
```

```python
import functools

import jax
import jax.numpy as jnp
from jax import lax
from jax.experimental import pallas as pl
from jax.experimental.pallas import tpu as pltpu
from jax.sharding import PartitionSpec as P

NZ = 64
SLOTS = 3
LANES = 128
EDGE = 3
F32 = jnp.float32
BF16 = jnp.bfloat16

VMEM = pl.BlockSpec(memory_space=pltpu.VMEM)
SMEM = pl.BlockSpec(memory_space=pltpu.SMEM)
HBM = pl.BlockSpec(memory_space=pltpu.HBM)


def params(mib):
    return pltpu.CompilerParams(vmem_limit_bytes=mib * 1024 * 1024)


def cost(flops, nbytes):
    return pl.CostEstimate(flops=flops, bytes_accessed=nbytes, transcendentals=0)


def in_hbm(array):
    return pltpu.with_memory_space_constraint(array, pltpu.HBM)


def split(value):
    high = value.astype(BF16)
    return high, (value - high.astype(F32)).astype(BF16)


def build_mix(mix, out_ref):
    zero = jnp.zeros((NZ, NZ), F32)
    pair = jnp.concatenate(
        [jnp.concatenate([mix, zero], axis=1), jnp.concatenate([zero, mix], axis=1)], axis=0
    )
    high, low = split(pair)
    out_ref[0:LANES, 0:LANES] = high
    out_ref[LANES:, 0:LANES] = high
    out_ref[0:LANES, LANES:] = low
    out_ref[LANES:, LANES:] = jnp.zeros((LANES, LANES), BF16)


def columns(tiles, taps):
    count = len(tiles)
    lower = lax.broadcasted_iota(jnp.int32, tiles[0].shape, 1) < NZ
    zero = jnp.zeros_like(tiles[0])
    turned = [pltpu.roll(tile, NZ, 1) for tile in tiles]
    between = {}
    for t in range(-1, count):
        first = turned[t] if t >= 0 else zero
        second = turned[t + 1] if t + 1 < count else zero
        between[t] = jnp.where(lower, first, second)
    outs = []
    for t in range(count):
        total = taps[3] * tiles[t]
        for k, at in ((1, t - 1), (5, t + 1)):
            if 0 <= at < count:
                total += taps[k] * tiles[at]
        for k, at in ((0, t - 2), (2, t - 1), (4, t), (6, t + 1)):
            if at in between:
                total += taps[k] * between[at]
        outs.append(total)
    return outs


def store_split(ref, stride, row, upper, lower):
    for t, (first, second) in enumerate(zip(upper, lower)):
        high, low = split(jnp.concatenate([first, second], axis=0))
        ref[stride * t + row : stride * t + row + 16, 0:LANES] = high
        ref[stride * t + row : stride * t + row + 16, LANES:] = low


def mixed(ref, start, size, matrix):
    both = jnp.dot(ref[start : start + size, :], matrix, preferred_element_type=F32)
    return both[:, 0:LANES] + both[:, LANES:]


def lanes_of(t):
    return slice(LANES * t, LANES * (t + 1))


def stage_kernel(perturb_hbm, mine_hbm, perturb_ref, mine_ref, border_ref, sems):
    members, _, rows, cells = perturb_ref.shape
    copies = []
    for member in range(members):
        copies.append(pltpu.make_async_copy(perturb_hbm.at[member], perturb_ref.at[member], sems.at[member]))
    copies.append(pltpu.make_async_copy(mine_hbm, mine_ref, sems.at[members]))
    for copy in copies:
        copy.start()
    for member in range(members):
        copies[member].wait()
        for slot in range(SLOTS):
            for t in range(cells // LANES):
                at = EDGE * (members * t + member)
                for side, start, first in ((0, 0, 0), (1, rows - 8, 8 - EDGE)):
                    value = perturb_ref[member, slot, start : start + 8, lanes_of(t)].astype(F32)
                    border_ref[slot, side, at : at + EDGE, :] = value[first : first + EDGE]
    copies[members].wait()


def by_parity(run, first, second):
    odd = lax.rem(lax.axis_index("tile"), 2) == 1
    pl.when(jnp.logical_not(odd))(lambda: run(first, second))
    pl.when(odd)(lambda: run(second, first))


def border_kernel(owner_ref, border_ref, mine_ref, other_ref, pair_ref, next_ref):
    by_parity(functools.partial(border_rows, owner_ref, border_ref, mine_ref, other_ref), pair_ref, next_ref)


def border_rows(owner_ref, border_ref, mine_ref, other_ref, up_ref, down_ref):
    _, _, rows, cells = mine_ref.shape
    total_rows = up_ref.shape[0]
    per_tile = total_rows // (cells // LANES)
    me = lax.axis_index("member")
    valid = [owner_ref[slot] == me for slot in range(SLOTS)]
    sublane = lax.broadcasted_iota(jnp.int32, (8, LANES), 0)
    phase = [lax.rem(sublane + shift, EDGE) for shift in range(EDGE)]
    is_zero = [value == 0 for value in phase]
    is_one = [value == 1 for value in phase]
    for start, ref, side in ((0, down_ref, 0), (rows - EDGE, up_ref, 1)):
        whole = {}
        for t in range(cells // LANES):
            for slot in range(SLOTS):
                lines = []
                for i in range(EDGE):
                    here = mine_ref[0, slot, start + i : start + i + 1, lanes_of(t)]
                    there = other_ref[0, slot, start + i : start + i + 1, lanes_of(t)]
                    lines.append(jnp.broadcast_to(jnp.where(valid[slot], here, there), (8, LANES)))
                for shift in range(EDGE):
                    whole[t, slot, shift] = jnp.where(
                        is_zero[shift], lines[0], jnp.where(is_one[shift], lines[1], lines[2])
                    )
            for row in range(0, total_rows, 8):
                if (row + 7) // per_tile != t:
                    continue
                total = None
                for slot in range(SLOTS):
                    field = whole[t, slot, row % EDGE]
                    if row // per_tile != t:
                        field = jnp.where(sublane < per_tile * t - row, whole[t - 1, slot, row % EDGE], field)
                    term = border_ref[slot, side, row : row + 8, :] * field
                    total = term if total is None else total + term
                ref[row : row + 8, :] = total


def bulk_kernel(
    owner_ref, taps_x_ref, taps_y_ref, mix_ref, perturb_ref, mine_ref, other_ref, control_hbm, velocity_hbm,
    local_ref, cross_pair_ref, cross_next_ref, square_ref, control_ref, velocity_ref,
    field, rows_of, left, turned, matrix, matrix_t, sems,
):
    members, _, rows, cells = perturb_ref.shape
    count = cells // LANES
    tall = rows + 16
    control_copy = pltpu.make_async_copy(control_hbm, control_ref, sems.at[0])
    velocity_copy = pltpu.make_async_copy(velocity_hbm, velocity_ref, sems.at[1])
    control_copy.start()
    velocity_copy.start()
    me = lax.axis_index("member")
    tile = lax.axis_index("tile")
    tiles = lax.axis_size("tile")
    taps_x = [taps_x_ref[k] for k in range(7)]
    taps_y = [taps_y_ref[k] for k in range(7)]
    build_mix(mix_ref[...], matrix)
    build_mix(mix_ref[...].T, matrix_t)
    for slot in range(SLOTS):
        field[slot] = jnp.where(owner_ref[slot] == me, mine_ref[0, slot], other_ref[0, slot])
    for half in range(2):
        rows_of[half, :, 0:8, :] = jnp.zeros((count, 8, LANES), F32)
        rows_of[half, :, tall - 8 : tall, :] = jnp.zeros((count, 8, LANES), F32)
    weight_top = jnp.where(tile > 0, 1.0, 0.0).astype(F32)
    weight_bottom = jnp.where(tile < tiles - 1, 1.0, 0.0).astype(F32)

    def pair_step(pair, carry):
        for half in range(2):
            member = 2 * pair + half
            for t in range(count):
                product = perturb_ref[member, 0, :, lanes_of(t)].astype(F32) * field[0, :, lanes_of(t)]
                for slot in range(1, SLOTS):
                    product += perturb_ref[member, slot, :, lanes_of(t)].astype(F32) * field[slot, :, lanes_of(t)]
                rows_of[half, t, 8 : 8 + rows, :] = product
        blocks = []
        for half in range(2):
            for row in range(0, tall, 8):
                used = range(7)
                if row == 0:
                    used = range(4, 7)
                if row == tall - 8:
                    used = range(0, 3)
                block = []
                for t in range(count):
                    total = None
                    for k in used:
                        term = taps_x[k] * rows_of[half, t, row + k - 3 : row + k + 5, :]
                        total = term if total is None else total + term
                    block.append(total)
                blocks.append(columns(block, taps_y))
                if len(blocks) == 2:
                    at = half * tall + row - 8
                    store_split(left, 2 * tall, at, *blocks)
                    blocks = []
        pl.when(pair == 0)(control_copy.wait)
        group = 4
        for first in range(0, count, group):
            size = 2 * tall
            out = mixed(left, size * first, size * group, matrix[...])
            for t in range(first, first + group):
                for half in range(2):
                    member = 2 * pair + half
                    base = size * (t - first) + tall * half
                    here = control_ref[member, :, lanes_of(t)] + out[base + 8 : base + 8 + rows]
                    local_ref[member, :, lanes_of(t)] = here
                    squared = here * here
                    for row in range(0, rows, 8):
                        carry += squared[row : row + 8]
                    above, below = out[base : base + 8], out[base + tall - 8 : base + tall]
                    carry += weight_top * (above * above) + weight_bottom * (below * below)
        return carry

    square_ref[...] = lax.fori_loop(0, members // 2, pair_step, jnp.zeros((8, LANES), F32))
    velocity_copy.wait()
    back = taps_y[::-1]

    def turn_step(pair, carry):
        for half in range(2):
            member = 2 * pair + half
            for t in range(count):
                rows_of[half, t, 8:16, :] = local_ref[member, 0:8, lanes_of(t)]
                rows_of[half, t, rows : rows + 8, :] = local_ref[member, rows - 8 : rows, lanes_of(t)]
        for half in range(2):
            first, last = [], []
            for t in range(count):
                total = taps_x[0] * rows_of[half, t, 8:16, :]
                other = taps_x[6] * rows_of[half, t, rows : rows + 8, :]
                for d in range(1, EDGE):
                    total += taps_x[d] * rows_of[half, t, 8 - d : 16 - d, :]
                    other += taps_x[6 - d] * rows_of[half, t, rows + d : rows + 8 + d, :]
                first.append(total)
                last.append(other)
            store_split(left, 32, 16 * half, columns(first, back), columns(last, back))
        out = mixed(left, 0, 32 * count, matrix_t[...])
        for t in range(count):
            for half in range(2):
                turned[2 * pair + half, t] = out[32 * t + 16 * half : 32 * t + 16 * half + 16]
        return carry

    lax.fori_loop(0, members // 2, turn_step, 0)

    def pack(cross_down_ref, cross_up_ref):
        for member in range(members):
            for t in range(count):
                at = EDGE * (members * t + member)
                cross_up_ref[at : at + EDGE, :] = turned[member, t, 0:EDGE, :]
                cross_down_ref[at : at + EDGE, :] = turned[member, t, 16 - EDGE : 16, :]

    by_parity(pack, cross_pair_ref, cross_next_ref)


def cross_kernel(square_ref, cross_pair_ref, cross_next_ref, from_pair_ref, from_next_ref, total_ref):
    total = [jnp.zeros((8, LANES), F32) for _ in range(4)]
    for step, row in enumerate(range(0, cross_pair_ref.shape[0], 8)):
        at = slice(row, row + 8)
        which = 2 * (step % 2)
        total[which] += cross_pair_ref[at] * from_pair_ref[at]
        total[which + 1] += cross_next_ref[at] * from_next_ref[at]
    total_ref[...] = square_ref[...] + 2.0 * ((total[0] + total[1]) + (total[2] + total[3]))


def correct_kernel(
    taps_x_ref, taps_y_ref, mix_ref, from_pair_ref, from_next_ref, local_ref, gradient_ref,
    rows_of, left, result, matrix,
):
    members, rows, cells = local_ref.shape
    count = cells // LANES
    here = EDGE * members
    taps_x = [taps_x_ref[k] for k in range(7)]
    taps_y = [taps_y_ref[k] for k in range(7)]
    build_mix(mix_ref[...], matrix)
    zero = jnp.zeros((8, LANES), F32)
    for t in range(count):
        rows_of[0, t, 24:32, :] = zero
        rows_of[0, t, 32:40, :] = zero
        rows_of[1, t, 0:8, :] = zero
        rows_of[1, t, 32:40, :] = zero

    def unpack(from_right_ref, from_left_ref):
        for t in range(count):
            rows_of[0, t, 0:here, :] = from_left_ref[here * t : here * (t + 1), :]
            rows_of[1, t, 8 : 8 + here, :] = from_right_ref[here * t : here * (t + 1), :]

    by_parity(unpack, from_pair_ref, from_next_ref)
    sublane = lax.broadcasted_iota(jnp.int32, (8, LANES), 0)
    blocks = []
    for side in range(2):
        for row in range(0, 32, 8):
            place = lax.rem(sublane + row, EDGE)
            if side == 0:
                factors = [jnp.where(place < EDGE - d, taps_x[d], 0.0) for d in range(EDGE)]
            else:
                factors = [jnp.where(place >= d, taps_x[6 - d], 0.0) for d in range(EDGE)]
            block = []
            for t in range(count):
                total = None
                for d in range(EDGE):
                    at = row + d if side == 0 else 8 + row - d
                    term = factors[d] * rows_of[side, t, at : at + 8, :]
                    total = term if total is None else total + term
                block.append(total)
            blocks.append(columns(block, taps_y))
            if len(blocks) == 2:
                store_split(left, 64, 32 * side + row - 8, *blocks)
                blocks = []
    group = 4
    for first in range(0, count, group):
        result[64 * first : 64 * (first + group), :] = mixed(left, 64 * first, 64 * group, matrix[...])
    for member in range(members):
        for t in range(count):
            at = 64 * t + EDGE * member
            gradient_ref[member, 0:EDGE, lanes_of(t)] += result[at : at + EDGE, :]
            gradient_ref[member, rows - EDGE : rows, lanes_of(t)] += result[at + 32 : at + 32 + EDGE, :]


def update_kernel(
    entries, near_ref, far_ref, control_ref, velocity_ref, gradient_ref,
    new_control_hbm, new_velocity_hbm, new_control, new_velocity, sems,
):
    members, rows, cells = control_ref.shape
    mean = jnp.sum(near_ref[...] + far_ref[...], keepdims=True) / entries
    scale = lax.rsqrt(mean + 1e-06)
    copies = []
    for member in range(members):
        for start in range(0, rows, 8):
            tile = slice(start, start + 8)
            moved = 0.9 * velocity_ref[member, tile] + scale * gradient_ref[member, tile]
            new_velocity[member, tile] = moved
            new_control[member, tile] = control_ref[member, tile] - 0.5 * moved
        for which, (src, dst) in enumerate(((new_control, new_control_hbm), (new_velocity, new_velocity_hbm))):
            copy = pltpu.make_async_copy(src.at[member], dst.at[member], sems.at[which, member])
            copy.start()
            copies.append(copy)
    for copy in copies:
        copy.wait()


def body(control, velocity, perturb, adjoint_forcing, slot_owner, taps_x, taps_y, vertical_mix):
    members, rows, cells = control.shape
    count = cells // LANES
    tiles = lax.axis_size("tile")
    groups = lax.axis_size("member")
    owner = slot_owner.reshape(SLOTS)
    swap = [(0, 1), (1, 0)]
    other = lax.ppermute(adjoint_forcing, "member", swap)
    edges = EDGE * members * count
    perturb, mine, border = pl.pallas_call(
        stage_kernel,
        name="stage",
        out_shape=(
            jax.ShapeDtypeStruct(perturb.shape, perturb.dtype),
            jax.ShapeDtypeStruct(adjoint_forcing.shape, F32),
            jax.ShapeDtypeStruct((SLOTS, 2, edges, LANES), F32),
        ),
        in_specs=[HBM, HBM],
        out_specs=(VMEM, VMEM, VMEM),
        scratch_shapes=[pltpu.SemaphoreType.DMA((members + 1,))],
        compiler_params=params(8),
        cost_estimate=cost(0, 8_000_000),
    )(in_hbm(perturb), in_hbm(adjoint_forcing))
    packed = jax.ShapeDtypeStruct((edges, LANES), F32)
    pair, after = pl.pallas_call(
        border_kernel,
        name="border_product",
        out_shape=(packed, packed),
        in_specs=[SMEM, VMEM, VMEM, VMEM],
        out_specs=(VMEM, VMEM),
        compiler_params=params(8),
        cost_estimate=cost(4_000_000, 4_000_000),
    )(owner, border, mine, other)
    swaps = [(i, i + 1) for i in range(tiles - 1)] + [(i + 1, i) for i in range(tiles - 1)]
    from_next = lax.ppermute(after, "tile", [(i, j) for i, j in swaps if min(i, j) % 2 == 1])
    from_pair = lax.ppermute(pair, "tile", [(i, j) for i, j in swaps if min(i, j) % 2 == 0])
    matrix = pltpu.VMEM((2 * LANES, 2 * LANES), BF16)
    whole = jax.ShapeDtypeStruct(control.shape, F32)
    local, cross_pair, cross_next, square, control, velocity = pl.pallas_call(
        bulk_kernel,
        name="bulk",
        out_shape=(whole, packed, packed, jax.ShapeDtypeStruct((8, LANES), F32), whole, whole),
        in_specs=[SMEM, SMEM, SMEM, VMEM, VMEM, VMEM, VMEM, HBM, HBM],
        out_specs=(VMEM,) * 6,
        scratch_shapes=[
            pltpu.VMEM((SLOTS, rows, cells), F32),
            pltpu.VMEM((2, count, rows + 16, LANES), F32),
            pltpu.VMEM((count * 2 * (rows + 16), 2 * LANES), BF16),
            pltpu.VMEM((members, count, 16, LANES), F32),
            matrix, matrix,
            pltpu.SemaphoreType.DMA((2,)),
        ],
        compiler_params=params(24),
        cost_estimate=cost(9_000_000_000, 12_000_000),
    )(owner, taps_x, taps_y, vertical_mix, perturb, mine, other, in_hbm(control), in_hbm(velocity))
    near = pl.pallas_call(
        cross_kernel,
        name="cross_term",
        out_shape=jax.ShapeDtypeStruct((8, LANES), F32),
        in_specs=[VMEM] * 5,
        out_specs=VMEM,
        compiler_params=params(8),
        cost_estimate=cost(200_000, 1_000_000),
    )(square, cross_pair, cross_next, from_pair, from_next)
    gradient = pl.pallas_call(
        correct_kernel,
        name="border_correction",
        out_shape=whole,
        in_specs=[SMEM, SMEM, VMEM, VMEM, VMEM, VMEM],
        out_specs=VMEM,
        scratch_shapes=[
            pltpu.VMEM((2, count, 40, LANES), F32),
            pltpu.VMEM((count * 64, 2 * LANES), BF16),
            pltpu.VMEM((count * 64, LANES), F32),
            matrix,
        ],
        input_output_aliases={5: 0},
        compiler_params=params(16),
        cost_estimate=cost(2_000_000_000, 2_000_000),
    )(taps_x, taps_y, vertical_mix, from_pair, from_next, local)
    steps = [("member", swap)]
    width = 1
    while width < tiles:
        steps.append(("tile", [(i, i ^ width) for i in range(tiles)]))
        width *= 2
    for axis, pairs in steps[:-1]:
        near = near + lax.ppermute(near, axis, pairs)
    far = lax.ppermute(near, *steps[-1])
    entries = members * groups * rows * tiles * cells
    return tuple(
        pl.pallas_call(
            functools.partial(update_kernel, float(entries)),
            name="update",
            out_shape=(whole, whole),
            in_specs=[VMEM] * 5,
            out_specs=(HBM, HBM),
            scratch_shapes=[
                pltpu.VMEM(control.shape, F32),
                pltpu.VMEM(control.shape, F32),
                pltpu.SemaphoreType.DMA((2, members)),
            ],
            compiler_params=params(16),
            cost_estimate=cost(3_000_000, 12_000_000),
        )(near, far, control, velocity, gradient)
    )


def solution(mesh):
    placed = (
        P(("window", "member"), "tile", None),
        P(("window", "member"), "tile", None),
        P(("window", "member"), None, "tile", None),
        P(("window", "member"), None, "tile", None),
        P("window", "tile"),
        P(),
        P(),
        P(),
    )
    return jax.shard_map(
        body,
        mesh=mesh,
        in_specs=placed,
        out_specs=(P(("window", "member"), "tile", None), P(("window", "member"), "tile", None)),
        check_vma=False,
    )
```

```python
import functools

import jax
import jax.numpy as jnp
from jax import lax
from jax.experimental import pallas as pl
from jax.experimental.pallas import tpu as pltpu
from jax.sharding import PartitionSpec as P

NZ = 64
SLOTS = 3
LANES = 128
EDGE = 3
F32 = jnp.float32
BF16 = jnp.bfloat16

VMEM = pl.BlockSpec(memory_space=pltpu.VMEM)
SMEM = pl.BlockSpec(memory_space=pltpu.SMEM)
HBM = pl.BlockSpec(memory_space=pltpu.HBM)


def params(mib):
    return pltpu.CompilerParams(vmem_limit_bytes=mib * 1024 * 1024)


def cost(flops, nbytes):
    return pl.CostEstimate(flops=flops, bytes_accessed=nbytes, transcendentals=0)


def in_hbm(array):
    return pltpu.with_memory_space_constraint(array, pltpu.HBM)


def split(value):
    high = value.astype(BF16)
    return high, (value - high.astype(F32)).astype(BF16)


def build_mix(mix, out_ref):
    zero = jnp.zeros((NZ, NZ), F32)
    pair = jnp.concatenate(
        [jnp.concatenate([mix, zero], axis=1), jnp.concatenate([zero, mix], axis=1)], axis=0
    )
    high, low = split(pair)
    out_ref[0:LANES, 0:LANES] = high
    out_ref[LANES:, 0:LANES] = high
    out_ref[0:LANES, LANES:] = low
    out_ref[LANES:, LANES:] = jnp.zeros((LANES, LANES), BF16)


def columns(tiles, taps):
    count = len(tiles)
    lower = lax.broadcasted_iota(jnp.int32, tiles[0].shape, 1) < NZ
    zero = jnp.zeros_like(tiles[0])
    turned = [pltpu.roll(tile, NZ, 1) for tile in tiles]
    between = {}
    for t in range(-1, count):
        first = turned[t] if t >= 0 else zero
        second = turned[t + 1] if t + 1 < count else zero
        between[t] = jnp.where(lower, first, second)
    outs = []
    for t in range(count):
        total = taps[3] * tiles[t]
        for k, at in ((1, t - 1), (5, t + 1)):
            if 0 <= at < count:
                total += taps[k] * tiles[at]
        for k, at in ((0, t - 2), (2, t - 1), (4, t), (6, t + 1)):
            if at in between:
                total += taps[k] * between[at]
        outs.append(total)
    return outs


def store_split(ref, stride, row, upper, lower):
    for t, (first, second) in enumerate(zip(upper, lower)):
        high, low = split(jnp.concatenate([first, second], axis=0))
        ref[stride * t + row : stride * t + row + 16, 0:LANES] = high
        ref[stride * t + row : stride * t + row + 16, LANES:] = low


def mixed(ref, start, size, matrix):
    both = jnp.dot(ref[start : start + size, :], matrix, preferred_element_type=F32)
    return both[:, 0:LANES] + both[:, LANES:]


def lanes_of(t):
    return slice(LANES * t, LANES * (t + 1))


def border_levels(rows_of, count, plain, lead, taps_y, left, matrix, result):
    sublane = lax.broadcasted_iota(jnp.int32, (8, LANES), 0)
    blocks = []
    for side in range(2):
        for row in range(0, 32, 8):
            place = lax.rem(sublane + row, EDGE)
            if side == 0:
                factors = [jnp.where(place < EDGE - d, plain[d], 0.0) for d in range(EDGE)]
            else:
                factors = [jnp.where(place >= d, lead[d], 0.0) for d in range(EDGE)]
            block = []
            for t in range(count):
                total = None
                for d in range(EDGE):
                    at = row + d if side == 0 else 8 + row - d
                    term = factors[d] * rows_of[side, t, at : at + 8, :]
                    total = term if total is None else total + term
                block.append(total)
            blocks.append(columns(block, taps_y))
            if len(blocks) == 2:
                store_split(left, 64, 32 * side + row - 8, *blocks)
                blocks = []
    group = 4
    for first in range(0, count, group):
        result[64 * first : 64 * (first + group), :] = mixed(left, 64 * first, 64 * group, matrix)


def clear_packed(rows_of, count):
    zero = jnp.zeros((8, LANES), F32)
    for t in range(count):
        rows_of[0, t, 24:32, :] = zero
        rows_of[0, t, 32:40, :] = zero
        rows_of[1, t, 0:8, :] = zero
        rows_of[1, t, 32:40, :] = zero


def stage_kernel(
    perturb_hbm, mine_hbm, mix_hbm, perturb_ref, mine_ref, border_ref, matrix_ref, matrix_t_ref, mix, sems
):
    members, _, rows, cells = perturb_ref.shape
    mix_copy = pltpu.make_async_copy(mix_hbm, mix, sems.at[members + 1])
    mix_copy.start()
    copies = []
    for member in range(members):
        copies.append(pltpu.make_async_copy(perturb_hbm.at[member], perturb_ref.at[member], sems.at[member]))
    copies.append(pltpu.make_async_copy(mine_hbm, mine_ref, sems.at[members]))
    for copy in copies:
        copy.start()
    mix_copy.wait()
    build_mix(mix[...], matrix_ref)
    build_mix(mix[...].T, matrix_t_ref)
    for member in range(members):
        copies[member].wait()
        for slot in range(SLOTS):
            for t in range(cells // LANES):
                at = EDGE * (members * t + member)
                for side, start, first in ((0, 0, 0), (1, rows - 8, 8 - EDGE)):
                    value = perturb_ref[member, slot, start : start + 8, lanes_of(t)].astype(F32)
                    border_ref[slot, side, at : at + EDGE, :] = value[first : first + EDGE]
    copies[members].wait()


def by_parity(run, first, second):
    odd = lax.rem(lax.axis_index("tile"), 2) == 1
    pl.when(jnp.logical_not(odd))(lambda: run(first, second))
    pl.when(odd)(lambda: run(second, first))


def border_kernel(owner_ref, border_ref, mine_ref, other_ref, pair_ref, next_ref):
    by_parity(functools.partial(border_rows, owner_ref, border_ref, mine_ref, other_ref), pair_ref, next_ref)


def border_rows(owner_ref, border_ref, mine_ref, other_ref, up_ref, down_ref):
    _, _, rows, cells = mine_ref.shape
    total_rows = up_ref.shape[0]
    per_tile = total_rows // (cells // LANES)
    me = lax.axis_index("member")
    valid = [owner_ref[slot] == me for slot in range(SLOTS)]
    sublane = lax.broadcasted_iota(jnp.int32, (8, LANES), 0)
    phase = [lax.rem(sublane + shift, EDGE) for shift in range(EDGE)]
    is_zero = [value == 0 for value in phase]
    is_one = [value == 1 for value in phase]
    for start, ref, side in ((0, down_ref, 0), (rows - EDGE, up_ref, 1)):
        whole = {}
        for t in range(cells // LANES):
            for slot in range(SLOTS):
                lines = []
                for i in range(EDGE):
                    here = mine_ref[0, slot, start + i : start + i + 1, lanes_of(t)]
                    there = other_ref[0, slot, start + i : start + i + 1, lanes_of(t)]
                    lines.append(jnp.broadcast_to(jnp.where(valid[slot], here, there), (8, LANES)))
                for shift in range(EDGE):
                    whole[t, slot, shift] = jnp.where(
                        is_zero[shift], lines[0], jnp.where(is_one[shift], lines[1], lines[2])
                    )
            for row in range(0, total_rows, 8):
                if (row + 7) // per_tile != t:
                    continue
                total = None
                for slot in range(SLOTS):
                    field = whole[t, slot, row % EDGE]
                    if row // per_tile != t:
                        field = jnp.where(sublane < per_tile * t - row, whole[t - 1, slot, row % EDGE], field)
                    term = border_ref[slot, side, row : row + 8, :] * field
                    total = term if total is None else total + term
                ref[row : row + 8, :] = total


def bulk_kernel(
    owner_ref, taps_x_ref, taps_y_ref, matrix, matrix_t, perturb_ref, mine_ref, other_ref, pair_ref, next_ref,
    control_hbm, velocity_hbm,
    local_ref, cross_pair_ref, cross_next_ref, square_ref, control_ref, velocity_ref,
    field, rows_of, packed, left, result, sems,
):
    members, _, rows, cells = perturb_ref.shape
    count = cells // LANES
    here = EDGE * members
    control_copy = pltpu.make_async_copy(control_hbm, control_ref, sems.at[0])
    velocity_copy = pltpu.make_async_copy(velocity_hbm, velocity_ref, sems.at[1])
    control_copy.start()
    velocity_copy.start()
    me = lax.axis_index("member")
    tile = lax.axis_index("tile")
    tiles = lax.axis_size("tile")
    taps_x = [taps_x_ref[k] for k in range(7)]
    taps_y = [taps_y_ref[k] for k in range(7)]
    first_taps, last_taps = taps_x[0:EDGE], taps_x[6 : 6 - EDGE : -1]
    for slot in range(SLOTS):
        field[slot] = jnp.where(owner_ref[slot] == me, mine_ref[0, slot], other_ref[0, slot])
    for half in range(2):
        rows_of[half, :, 0:8, :] = jnp.zeros((count, 8, LANES), F32)
        rows_of[half, :, rows + 8 : rows + 16, :] = jnp.zeros((count, 8, LANES), F32)
    clear_packed(packed, count)

    def unpack(up_ref, down_ref):
        for t in range(count):
            packed[0, t, 0:here, :] = up_ref[here * t : here * (t + 1), :]
            packed[1, t, 8 : 8 + here, :] = down_ref[here * t : here * (t + 1), :]

    by_parity(unpack, pair_ref, next_ref)
    border_levels(packed, count, first_taps, last_taps, taps_y, left, matrix[...], result)
    weights = [jnp.where(tile < tiles - 1, 1.0, 0.0).astype(F32), jnp.where(tile > 0, 1.0, 0.0).astype(F32)]
    squares = jnp.zeros((8, LANES), F32)
    for side in range(2):
        total = [jnp.zeros((8, LANES), F32) for _ in range(4)]
        for t in range(count):
            for step in range(4):
                value = result[64 * t + 32 * side + 8 * step : 64 * t + 32 * side + 8 * step + 8, :]
                total[step] += value * value
        squares += weights[side] * ((total[0] + total[1]) + (total[2] + total[3]))

    def pair_step(pair, carry):
        for half in range(2):
            member = 2 * pair + half
            for t in range(count):
                product = perturb_ref[member, 0, :, lanes_of(t)].astype(F32) * field[0, :, lanes_of(t)]
                for slot in range(1, SLOTS):
                    product += perturb_ref[member, slot, :, lanes_of(t)].astype(F32) * field[slot, :, lanes_of(t)]
                rows_of[half, t, 8 : 8 + rows, :] = product
        blocks = []
        size = 2 * rows
        for half in range(2):
            for row in range(0, rows, 8):
                block = []
                for t in range(count):
                    total = None
                    for k in range(7):
                        term = taps_x[k] * rows_of[half, t, row + k + 5 : row + k + 13, :]
                        total = term if total is None else total + term
                    block.append(total)
                blocks.append(columns(block, taps_y))
                if len(blocks) == 2:
                    store_split(left, size, half * rows + row - 8, *blocks)
                    blocks = []
        pl.when(pair == 0)(control_copy.wait)
        group = 4
        for first in range(0, count, group):
            out = mixed(left, size * first, size * group, matrix[...])
            for t in range(first, first + group):
                for half in range(2):
                    member = 2 * pair + half
                    base = size * (t - first) + rows * half
                    value = control_ref[member, :, lanes_of(t)] + out[base : base + rows]
                    local_ref[member, :, lanes_of(t)] = value
                    squared = value * value
                    for row in range(0, rows, 8):
                        carry += squared[row : row + 8]
                    packed[0, t, pl.ds(EDGE * member, EDGE), :] = value[rows - EDGE : rows]
                    packed[1, t, pl.ds(8 + EDGE * member, EDGE), :] = value[0:EDGE]
        return carry

    square_ref[...] = lax.fori_loop(0, members // 2, pair_step, squares)
    velocity_copy.wait()
    border_levels(packed, count, last_taps, first_taps, taps_y[::-1], left, matrix_t[...], result)

    def pack(cross_down_ref, cross_up_ref):
        for t in range(count):
            cross_down_ref[here * t : here * (t + 1), :] = result[64 * t : 64 * t + here, :]
            cross_up_ref[here * t : here * (t + 1), :] = result[64 * t + 32 : 64 * t + 32 + here, :]

    by_parity(pack, cross_pair_ref, cross_next_ref)


def cross_kernel(square_ref, cross_pair_ref, cross_next_ref, from_pair_ref, from_next_ref, total_ref):
    total = [jnp.zeros((8, LANES), F32) for _ in range(4)]
    for step, row in enumerate(range(0, cross_pair_ref.shape[0], 8)):
        at = slice(row, row + 8)
        which = 2 * (step % 2)
        total[which] += cross_pair_ref[at] * from_pair_ref[at]
        total[which + 1] += cross_next_ref[at] * from_next_ref[at]
    total_ref[...] = square_ref[...] + 2.0 * ((total[0] + total[1]) + (total[2] + total[3]))


def correct_kernel(
    taps_x_ref, taps_y_ref, matrix, from_pair_ref, from_next_ref, local_ref, gradient_ref, packed, left, result
):
    members, rows, cells = local_ref.shape
    count = cells // LANES
    here = EDGE * members
    taps_x = [taps_x_ref[k] for k in range(7)]
    taps_y = [taps_y_ref[k] for k in range(7)]
    clear_packed(packed, count)

    def unpack(from_right_ref, from_left_ref):
        for t in range(count):
            packed[0, t, 0:here, :] = from_left_ref[here * t : here * (t + 1), :]
            packed[1, t, 8 : 8 + here, :] = from_right_ref[here * t : here * (t + 1), :]

    by_parity(unpack, from_pair_ref, from_next_ref)
    border_levels(
        packed, count, taps_x[0:EDGE], taps_x[6 : 6 - EDGE : -1], taps_y, left, matrix[...], result
    )
    for member in range(members):
        for t in range(count):
            at = 64 * t + EDGE * member
            gradient_ref[member, 0:EDGE, lanes_of(t)] += result[at : at + EDGE, :]
            gradient_ref[member, rows - EDGE : rows, lanes_of(t)] += result[at + 32 : at + 32 + EDGE, :]


def update_kernel(
    entries, near_ref, far_ref, control_ref, velocity_ref, gradient_ref,
    new_control_hbm, new_velocity_hbm, new_control, new_velocity, sems,
):
    members, rows, cells = control_ref.shape
    mean = jnp.sum(near_ref[...] + far_ref[...], keepdims=True) / entries
    scale = lax.rsqrt(mean + 1e-06)
    copies = []
    for member in range(members):
        for start in range(0, rows, 8):
            tile = slice(start, start + 8)
            moved = 0.9 * velocity_ref[member, tile] + scale * gradient_ref[member, tile]
            new_velocity[member, tile] = moved
            new_control[member, tile] = control_ref[member, tile] - 0.5 * moved
        for which, (src, dst) in enumerate(((new_control, new_control_hbm), (new_velocity, new_velocity_hbm))):
            copy = pltpu.make_async_copy(src.at[member], dst.at[member], sems.at[which, member])
            copy.start()
            copies.append(copy)
    for copy in copies:
        copy.wait()


def body(control, velocity, perturb, adjoint_forcing, slot_owner, taps_x, taps_y, vertical_mix):
    members, rows, cells = control.shape
    count = cells // LANES
    tiles = lax.axis_size("tile")
    groups = lax.axis_size("member")
    owner = slot_owner.reshape(SLOTS)
    swap = [(0, 1), (1, 0)]
    other = lax.ppermute(adjoint_forcing, "member", swap)
    edges = EDGE * members * count
    square_matrix = (2 * LANES, 2 * LANES)
    perturb, mine, border, matrix, matrix_t = pl.pallas_call(
        stage_kernel,
        name="stage",
        out_shape=(
            jax.ShapeDtypeStruct(perturb.shape, perturb.dtype),
            jax.ShapeDtypeStruct(adjoint_forcing.shape, F32),
            jax.ShapeDtypeStruct((SLOTS, 2, edges, LANES), F32),
            jax.ShapeDtypeStruct(square_matrix, BF16),
            jax.ShapeDtypeStruct(square_matrix, BF16),
        ),
        in_specs=[HBM, HBM, HBM],
        out_specs=(VMEM,) * 5,
        scratch_shapes=[pltpu.VMEM(vertical_mix.shape, F32), pltpu.SemaphoreType.DMA((members + 2,))],
        compiler_params=params(8),
        cost_estimate=cost(0, 8_000_000),
    )(in_hbm(perturb), in_hbm(adjoint_forcing), in_hbm(vertical_mix))
    packed = jax.ShapeDtypeStruct((edges, LANES), F32)
    pair, after = pl.pallas_call(
        border_kernel,
        name="border_product",
        out_shape=(packed, packed),
        in_specs=[SMEM, VMEM, VMEM, VMEM],
        out_specs=(VMEM, VMEM),
        compiler_params=params(8),
        cost_estimate=cost(4_000_000, 4_000_000),
    )(owner, border, mine, other)
    swaps = [(i, i + 1) for i in range(tiles - 1)] + [(i + 1, i) for i in range(tiles - 1)]
    from_next = lax.ppermute(after, "tile", [(i, j) for i, j in swaps if min(i, j) % 2 == 1])
    from_pair = lax.ppermute(pair, "tile", [(i, j) for i, j in swaps if min(i, j) % 2 == 0])
    border_scratch = [
        pltpu.VMEM((2, count, 40, LANES), F32),
        pltpu.VMEM((count * 64, 2 * LANES), BF16),
        pltpu.VMEM((count * 64, LANES), F32),
    ]
    whole = jax.ShapeDtypeStruct(control.shape, F32)
    local, cross_pair, cross_next, square, control, velocity = pl.pallas_call(
        bulk_kernel,
        name="bulk",
        out_shape=(whole, packed, packed, jax.ShapeDtypeStruct((8, LANES), F32), whole, whole),
        in_specs=[SMEM, SMEM, SMEM] + [VMEM] * 7 + [HBM, HBM],
        out_specs=(VMEM,) * 6,
        scratch_shapes=[
            pltpu.VMEM((SLOTS, rows, cells), F32),
            pltpu.VMEM((2, count, rows + 16, LANES), F32),
            *border_scratch,
            pltpu.SemaphoreType.DMA((2,)),
        ],
        compiler_params=params(24),
        cost_estimate=cost(9_000_000_000, 12_000_000),
    )(
        owner, taps_x, taps_y, matrix, matrix_t, perturb, mine, other, pair, after,
        in_hbm(control), in_hbm(velocity),
    )
    near = pl.pallas_call(
        cross_kernel,
        name="cross_term",
        out_shape=jax.ShapeDtypeStruct((8, LANES), F32),
        in_specs=[VMEM] * 5,
        out_specs=VMEM,
        compiler_params=params(8),
        cost_estimate=cost(200_000, 1_000_000),
    )(square, cross_pair, cross_next, from_pair, from_next)
    gradient = pl.pallas_call(
        correct_kernel,
        name="border_correction",
        out_shape=whole,
        in_specs=[SMEM, SMEM, VMEM, VMEM, VMEM, VMEM],
        out_specs=VMEM,
        scratch_shapes=border_scratch,
        input_output_aliases={5: 0},
        compiler_params=params(16),
        cost_estimate=cost(2_000_000_000, 2_000_000),
    )(taps_x, taps_y, matrix, from_pair, from_next, local)
    steps = [("member", swap)]
    width = 1
    while width < tiles:
        steps.append(("tile", [(i, i ^ width) for i in range(tiles)]))
        width *= 2
    for axis, pairs in steps[:-1]:
        near = near + lax.ppermute(near, axis, pairs)
    far = lax.ppermute(near, *steps[-1])
    entries = members * groups * rows * tiles * cells
    return tuple(
        pl.pallas_call(
            functools.partial(update_kernel, float(entries)),
            name="update",
            out_shape=(whole, whole),
            in_specs=[VMEM] * 5,
            out_specs=(HBM, HBM),
            scratch_shapes=[
                pltpu.VMEM(control.shape, F32),
                pltpu.VMEM(control.shape, F32),
                pltpu.SemaphoreType.DMA((2, members)),
            ],
            compiler_params=params(16),
            cost_estimate=cost(3_000_000, 12_000_000),
        )(near, far, control, velocity, gradient)
    )


def solution(mesh):
    placed = (
        P(("window", "member"), "tile", None),
        P(("window", "member"), "tile", None),
        P(("window", "member"), None, "tile", None),
        P(("window", "member"), None, "tile", None),
        P("window", "tile"),
        P(),
        P(),
        P(),
    )
    return jax.shard_map(
        body,
        mesh=mesh,
        in_specs=placed,
        out_specs=(P(("window", "member"), "tile", None), P(("window", "member"), "tile", None)),
        check_vma=False,
    )
```

```python
import functools

import jax
import jax.numpy as jnp
from jax import lax
from jax.experimental import pallas as pl
from jax.experimental.pallas import tpu as pltpu
from jax.sharding import PartitionSpec as P

NZ = 64
SLOTS = 3
LANES = 128
EDGE = 3
F32 = jnp.float32
BF16 = jnp.bfloat16

VMEM = pl.BlockSpec(memory_space=pltpu.VMEM)
SMEM = pl.BlockSpec(memory_space=pltpu.SMEM)
HBM = pl.BlockSpec(memory_space=pltpu.HBM)


def params(mib):
    return pltpu.CompilerParams(vmem_limit_bytes=mib * 1024 * 1024)


def cost(flops, nbytes):
    return pl.CostEstimate(flops=flops, bytes_accessed=nbytes, transcendentals=0)


def in_hbm(array):
    return pltpu.with_memory_space_constraint(array, pltpu.HBM)


def split(value):
    high = value.astype(BF16)
    return high, (value - high.astype(F32)).astype(BF16)


def build_mix(mix, out_ref):
    zero = jnp.zeros((NZ, NZ), F32)
    pair = jnp.concatenate(
        [jnp.concatenate([mix, zero], axis=1), jnp.concatenate([zero, mix], axis=1)], axis=0
    )
    high, low = split(pair)
    out_ref[0:LANES, 0:LANES] = high
    out_ref[LANES:, 0:LANES] = high
    out_ref[0:LANES, LANES:] = low
    out_ref[LANES:, LANES:] = jnp.zeros((LANES, LANES), BF16)


def columns(tiles, taps):
    count = len(tiles)
    lower = lax.broadcasted_iota(jnp.int32, tiles[0].shape, 1) < NZ
    zero = jnp.zeros_like(tiles[0])
    turned = [pltpu.roll(tile, NZ, 1) for tile in tiles]
    between = {}
    for t in range(-1, count):
        first = turned[t] if t >= 0 else zero
        second = turned[t + 1] if t + 1 < count else zero
        between[t] = jnp.where(lower, first, second)
    outs = []
    for t in range(count):
        total = taps[3] * tiles[t]
        for k, at in ((1, t - 1), (5, t + 1)):
            if 0 <= at < count:
                total += taps[k] * tiles[at]
        for k, at in ((0, t - 2), (2, t - 1), (4, t), (6, t + 1)):
            if at in between:
                total += taps[k] * between[at]
        outs.append(total)
    return outs


def store_split(ref, stride, row, upper, lower):
    for t, (first, second) in enumerate(zip(upper, lower)):
        high, low = split(jnp.concatenate([first, second], axis=0))
        ref[stride * t + row : stride * t + row + 16, 0:LANES] = high
        ref[stride * t + row : stride * t + row + 16, LANES:] = low


def mixed(ref, start, size, matrix):
    both = jnp.dot(ref[start : start + size, :], matrix, preferred_element_type=F32)
    return both[:, 0:LANES] + both[:, LANES:]


def lanes_of(t):
    return slice(LANES * t, LANES * (t + 1))


def border_levels(rows_of, count, plain, lead, taps_y, left, matrix, result):
    sublane = lax.broadcasted_iota(jnp.int32, (8, LANES), 0)
    blocks = []
    for side in range(2):
        for row in range(0, 32, 8):
            place = lax.rem(sublane + row, EDGE)
            if side == 0:
                factors = [jnp.where(place < EDGE - d, plain[d], 0.0) for d in range(EDGE)]
            else:
                factors = [jnp.where(place >= d, lead[d], 0.0) for d in range(EDGE)]
            block = []
            for t in range(count):
                total = None
                for d in range(EDGE):
                    at = row + d if side == 0 else 8 + row - d
                    term = factors[d] * rows_of[side, t, at : at + 8, :]
                    total = term if total is None else total + term
                block.append(total)
            blocks.append(columns(block, taps_y))
            if len(blocks) == 2:
                store_split(left, 64, 32 * side + row - 8, *blocks)
                blocks = []
    group = 4
    for first in range(0, count, group):
        result[64 * first : 64 * (first + group), :] = mixed(left, 64 * first, 64 * group, matrix)


def clear_packed(rows_of, count):
    zero = jnp.zeros((8, LANES), F32)
    for t in range(count):
        rows_of[0, t, 24:32, :] = zero
        rows_of[0, t, 32:40, :] = zero
        rows_of[1, t, 0:8, :] = zero
        rows_of[1, t, 32:40, :] = zero


def stage_kernel(
    perturb_hbm, mine_hbm, mix_hbm, perturb_ref, mine_ref, border_ref, matrix_ref, matrix_t_ref, mix, sems
):
    members, _, rows, cells = perturb_ref.shape
    mix_copy = pltpu.make_async_copy(mix_hbm, mix, sems.at[members + 1])
    mix_copy.start()
    copies = []
    for member in range(members):
        copies.append(pltpu.make_async_copy(perturb_hbm.at[member], perturb_ref.at[member], sems.at[member]))
    copies.append(pltpu.make_async_copy(mine_hbm, mine_ref, sems.at[members]))
    for copy in copies:
        copy.start()
    mix_copy.wait()
    build_mix(mix[...], matrix_ref)
    build_mix(mix[...].T, matrix_t_ref)
    for member in range(members):
        copies[member].wait()
        for slot in range(SLOTS):
            for t in range(cells // LANES):
                at = EDGE * (members * t + member)
                for side, start, first in ((0, 0, 0), (1, rows - 8, 8 - EDGE)):
                    value = perturb_ref[member, slot, start : start + 8, lanes_of(t)].astype(F32)
                    border_ref[slot, side, at : at + EDGE, :] = value[first : first + EDGE]
    copies[members].wait()


def by_parity(run, first, second):
    odd = lax.rem(lax.axis_index("tile"), 2) == 1
    pl.when(jnp.logical_not(odd))(lambda: run(first, second))
    pl.when(odd)(lambda: run(second, first))


def border_kernel(owner_ref, border_ref, mine_ref, other_ref, pair_ref, next_ref):
    by_parity(functools.partial(border_rows, owner_ref, border_ref, mine_ref, other_ref), pair_ref, next_ref)


def border_rows(owner_ref, border_ref, mine_ref, other_ref, up_ref, down_ref):
    _, _, rows, cells = mine_ref.shape
    total_rows = up_ref.shape[0]
    per_tile = total_rows // (cells // LANES)
    me = lax.axis_index("member")
    valid = [owner_ref[slot] == me for slot in range(SLOTS)]
    sublane = lax.broadcasted_iota(jnp.int32, (8, LANES), 0)
    phase = [lax.rem(sublane + shift, EDGE) for shift in range(EDGE)]
    is_zero = [value == 0 for value in phase]
    is_one = [value == 1 for value in phase]
    for start, ref, side in ((0, down_ref, 0), (rows - EDGE, up_ref, 1)):
        whole = {}
        for t in range(cells // LANES):
            for slot in range(SLOTS):
                lines = []
                for i in range(EDGE):
                    here = mine_ref[0, slot, start + i : start + i + 1, lanes_of(t)]
                    there = other_ref[0, slot, start + i : start + i + 1, lanes_of(t)]
                    lines.append(jnp.broadcast_to(jnp.where(valid[slot], here, there), (8, LANES)))
                for shift in range(EDGE):
                    whole[t, slot, shift] = jnp.where(
                        is_zero[shift], lines[0], jnp.where(is_one[shift], lines[1], lines[2])
                    )
            for row in range(0, total_rows, 8):
                if (row + 7) // per_tile != t:
                    continue
                total = None
                for slot in range(SLOTS):
                    field = whole[t, slot, row % EDGE]
                    if row // per_tile != t:
                        field = jnp.where(sublane < per_tile * t - row, whole[t - 1, slot, row % EDGE], field)
                    term = border_ref[slot, side, row : row + 8, :] * field
                    total = term if total is None else total + term
                ref[row : row + 8, :] = total


def bulk_kernel(
    owner_ref, taps_x_ref, taps_y_ref, matrix, matrix_t, perturb_ref, mine_ref, other_ref, pair_ref, next_ref,
    control_hbm, velocity_hbm,
    local_ref, cross_pair_ref, cross_next_ref, square_ref, control_ref, velocity_ref,
    field, rows_of, packed, left, result, sems,
):
    members, _, rows, cells = perturb_ref.shape
    count = cells // LANES
    here = EDGE * members
    control_copy = pltpu.make_async_copy(control_hbm, control_ref, sems.at[0])
    velocity_copy = pltpu.make_async_copy(velocity_hbm, velocity_ref, sems.at[1])
    control_copy.start()
    velocity_copy.start()
    me = lax.axis_index("member")
    tile = lax.axis_index("tile")
    tiles = lax.axis_size("tile")
    taps_x = [taps_x_ref[k] for k in range(7)]
    taps_y = [taps_y_ref[k] for k in range(7)]
    first_taps, last_taps = taps_x[0:EDGE], taps_x[6 : 6 - EDGE : -1]
    for slot in range(SLOTS):
        field[slot] = jnp.where(owner_ref[slot] == me, mine_ref[0, slot], other_ref[0, slot])
    for half in range(2):
        rows_of[half, :, 0:8, :] = jnp.zeros((count, 8, LANES), F32)
        rows_of[half, :, rows + 8 : rows + 16, :] = jnp.zeros((count, 8, LANES), F32)
    clear_packed(packed, count)

    def unpack(up_ref, down_ref):
        for t in range(count):
            packed[0, t, 0:here, :] = up_ref[here * t : here * (t + 1), :]
            packed[1, t, 8 : 8 + here, :] = down_ref[here * t : here * (t + 1), :]

    by_parity(unpack, pair_ref, next_ref)
    border_levels(packed, count, first_taps, last_taps, taps_y, left, matrix[...], result)
    weights = [jnp.where(tile < tiles - 1, 1.0, 0.0).astype(F32), jnp.where(tile > 0, 1.0, 0.0).astype(F32)]
    squares = jnp.zeros((8, LANES), F32)
    for side in range(2):
        total = [jnp.zeros((8, LANES), F32) for _ in range(4)]
        for t in range(count):
            for step in range(4):
                value = result[64 * t + 32 * side + 8 * step : 64 * t + 32 * side + 8 * step + 8, :]
                total[step] += value * value
        squares += weights[side] * ((total[0] + total[1]) + (total[2] + total[3]))

    def pair_step(pair, carry):
        for half in range(2):
            member = 2 * pair + half
            for t in range(count):
                product = perturb_ref[member, 0, :, lanes_of(t)].astype(F32) * field[0, :, lanes_of(t)]
                for slot in range(1, SLOTS):
                    product += perturb_ref[member, slot, :, lanes_of(t)].astype(F32) * field[slot, :, lanes_of(t)]
                rows_of[half, t, 8 : 8 + rows, :] = product
        blocks = []
        size = 2 * rows
        for half in range(2):
            for row in range(0, rows, 8):
                block = []
                for t in range(count):
                    total = None
                    for k in range(7):
                        term = taps_x[k] * rows_of[half, t, row + k + 5 : row + k + 13, :]
                        total = term if total is None else total + term
                    block.append(total)
                blocks.append(columns(block, taps_y))
                if len(blocks) == 2:
                    store_split(left, size, half * rows + row - 8, *blocks)
                    blocks = []
        pl.when(pair == 0)(control_copy.wait)
        group = 4
        for first in range(0, count, group):
            out = mixed(left, size * first, size * group, matrix[...])
            for t in range(first, first + group):
                for half in range(2):
                    member = 2 * pair + half
                    base = size * (t - first) + rows * half
                    value = control_ref[member, :, lanes_of(t)] + out[base : base + rows]
                    local_ref[member, :, lanes_of(t)] = value
                    squared = value * value
                    for row in range(0, rows, 8):
                        carry += squared[row : row + 8]
                    packed[0, t, pl.ds(EDGE * member, EDGE), :] = value[rows - EDGE : rows]
                    packed[1, t, pl.ds(8 + EDGE * member, EDGE), :] = value[0:EDGE]
        return carry

    square_ref[...] = lax.fori_loop(0, members // 2, pair_step, squares)
    velocity_copy.wait()
    border_levels(packed, count, last_taps, first_taps, taps_y[::-1], left, matrix_t[...], result)

    def pack(cross_down_ref, cross_up_ref):
        for t in range(count):
            cross_down_ref[here * t : here * (t + 1), :] = result[64 * t : 64 * t + here, :]
            cross_up_ref[here * t : here * (t + 1), :] = result[64 * t + 32 : 64 * t + 32 + here, :]

    by_parity(pack, cross_pair_ref, cross_next_ref)


def cross_kernel(square_ref, cross_pair_ref, cross_next_ref, from_pair_ref, from_next_ref, total_ref):
    total = [jnp.zeros((8, LANES), F32) for _ in range(4)]
    for step, row in enumerate(range(0, cross_pair_ref.shape[0], 8)):
        at = slice(row, row + 8)
        which = 2 * (step % 2)
        total[which] += cross_pair_ref[at] * from_pair_ref[at]
        total[which + 1] += cross_next_ref[at] * from_next_ref[at]
    total_ref[...] = square_ref[...] + 2.0 * ((total[0] + total[1]) + (total[2] + total[3]))


def correct_kernel(
    taps_x_ref, taps_y_ref, matrix, from_pair_ref, from_next_ref, local_ref, gradient_ref, packed, left, result
):
    members, rows, cells = local_ref.shape
    count = cells // LANES
    here = EDGE * members
    taps_x = [taps_x_ref[k] for k in range(7)]
    taps_y = [taps_y_ref[k] for k in range(7)]
    clear_packed(packed, count)

    def unpack(from_right_ref, from_left_ref):
        for t in range(count):
            packed[0, t, 0:here, :] = from_left_ref[here * t : here * (t + 1), :]
            packed[1, t, 8 : 8 + here, :] = from_right_ref[here * t : here * (t + 1), :]

    by_parity(unpack, from_pair_ref, from_next_ref)
    border_levels(
        packed, count, taps_x[0:EDGE], taps_x[6 : 6 - EDGE : -1], taps_y, left, matrix[...], result
    )
    for member in range(members):
        for t in range(count):
            at = 64 * t + EDGE * member
            gradient_ref[member, 0:EDGE, lanes_of(t)] += result[at : at + EDGE, :]
            gradient_ref[member, rows - EDGE : rows, lanes_of(t)] += result[at + 32 : at + 32 + EDGE, :]


def update_kernel(
    entries, near_ref, far_ref, control_ref, velocity_ref, gradient_ref,
    new_control_hbm, new_velocity_hbm, new_control, new_velocity, sems,
):
    members, rows, cells = control_ref.shape
    mean = jnp.sum(near_ref[...] + far_ref[...], keepdims=True) / entries
    scale = lax.rsqrt(mean + 1e-06)
    copies = []
    for member in range(members):
        for start in range(0, rows, 8):
            tile = slice(start, start + 8)
            moved = 0.9 * velocity_ref[member, tile] + scale * gradient_ref[member, tile]
            new_velocity[member, tile] = moved
            new_control[member, tile] = control_ref[member, tile] - 0.5 * moved
        for which, (src, dst) in enumerate(((new_control, new_control_hbm), (new_velocity, new_velocity_hbm))):
            copy = pltpu.make_async_copy(src.at[member], dst.at[member], sems.at[which, member])
            copy.start()
            copies.append(copy)
    for copy in copies:
        copy.wait()


def body(control, velocity, perturb, adjoint_forcing, slot_owner, taps_x, taps_y, vertical_mix):
    members, rows, cells = control.shape
    count = cells // LANES
    tiles = lax.axis_size("tile")
    groups = lax.axis_size("member")
    owner = slot_owner.reshape(SLOTS)
    swap = [(0, 1), (1, 0)]
    other = lax.ppermute(adjoint_forcing, "member", swap)
    edges = EDGE * members * count
    square_matrix = (2 * LANES, 2 * LANES)
    perturb, mine, border, matrix, matrix_t = pl.pallas_call(
        stage_kernel,
        name="stage",
        out_shape=(
            jax.ShapeDtypeStruct(perturb.shape, perturb.dtype),
            jax.ShapeDtypeStruct(adjoint_forcing.shape, F32),
            jax.ShapeDtypeStruct((SLOTS, 2, edges, LANES), F32),
            jax.ShapeDtypeStruct(square_matrix, BF16),
            jax.ShapeDtypeStruct(square_matrix, BF16),
        ),
        in_specs=[HBM, HBM, HBM],
        out_specs=(VMEM,) * 5,
        scratch_shapes=[pltpu.VMEM(vertical_mix.shape, F32), pltpu.SemaphoreType.DMA((members + 2,))],
        compiler_params=params(8),
        cost_estimate=cost(0, 8_000_000),
    )(in_hbm(perturb), in_hbm(adjoint_forcing), in_hbm(vertical_mix))
    packed = jax.ShapeDtypeStruct((edges, LANES), F32)
    pair, after = pl.pallas_call(
        border_kernel,
        name="border_product",
        out_shape=(packed, packed),
        in_specs=[SMEM, VMEM, VMEM, VMEM],
        out_specs=(VMEM, VMEM),
        compiler_params=params(8),
        cost_estimate=cost(4_000_000, 4_000_000),
    )(owner, border, mine, other)
    swaps = [(i, i + 1) for i in range(tiles - 1)] + [(i + 1, i) for i in range(tiles - 1)]
    from_next = lax.ppermute(after, "tile", [(i, j) for i, j in swaps if min(i, j) % 2 == 1])
    from_pair = lax.ppermute(pair, "tile", [(i, j) for i, j in swaps if min(i, j) % 2 == 0])
    border_scratch = [
        pltpu.VMEM((2, count, 40, LANES), F32),
        pltpu.VMEM((count * 64, 2 * LANES), BF16),
        pltpu.VMEM((count * 64, LANES), F32),
    ]
    whole = jax.ShapeDtypeStruct(control.shape, F32)
    local, cross_pair, cross_next, square, control, velocity = pl.pallas_call(
        bulk_kernel,
        name="bulk",
        out_shape=(whole, packed, packed, jax.ShapeDtypeStruct((8, LANES), F32), whole, whole),
        in_specs=[SMEM, SMEM, SMEM] + [VMEM] * 7 + [HBM, HBM],
        out_specs=(VMEM,) * 6,
        scratch_shapes=[
            pltpu.VMEM((SLOTS, rows, cells), F32),
            pltpu.VMEM((2, count, rows + 16, LANES), F32),
            *border_scratch,
            pltpu.SemaphoreType.DMA((2,)),
        ],
        compiler_params=params(24),
        cost_estimate=cost(9_000_000_000, 12_000_000),
    )(
        owner, taps_x, taps_y, matrix, matrix_t, perturb, mine, other, pair, after,
        in_hbm(control), in_hbm(velocity),
    )
    near = pl.pallas_call(
        cross_kernel,
        name="cross_term",
        out_shape=jax.ShapeDtypeStruct((8, LANES), F32),
        in_specs=[VMEM] * 5,
        out_specs=VMEM,
        compiler_params=params(8),
        cost_estimate=cost(200_000, 1_000_000),
    )(square, cross_pair, cross_next, from_pair, from_next)
    gradient = pl.pallas_call(
        correct_kernel,
        name="border_correction",
        out_shape=whole,
        in_specs=[SMEM, SMEM, VMEM, VMEM, VMEM, VMEM],
        out_specs=VMEM,
        scratch_shapes=border_scratch,
        input_output_aliases={5: 0},
        compiler_params=params(16),
        cost_estimate=cost(2_000_000_000, 2_000_000),
    )(taps_x, taps_y, matrix, from_pair, from_next, local)
    near = near + lax.ppermute(near, "member", swap)
    steps = []
    width = 1
    while width < tiles:
        steps.append([(groups * i + g, groups * (i ^ width) + groups - 1 - g) for i in range(tiles) for g in range(groups)])
        width *= 2
    for pairs in steps[:-1]:
        near = near + lax.ppermute(near, ("tile", "member"), pairs)
    far = lax.ppermute(near, ("tile", "member"), steps[-1])
    entries = members * groups * rows * tiles * cells
    return tuple(
        pl.pallas_call(
            functools.partial(update_kernel, float(entries)),
            name="update",
            out_shape=(whole, whole),
            in_specs=[VMEM] * 5,
            out_specs=(HBM, HBM),
            scratch_shapes=[
                pltpu.VMEM(control.shape, F32),
                pltpu.VMEM(control.shape, F32),
                pltpu.SemaphoreType.DMA((2, members)),
            ],
            compiler_params=params(16),
            cost_estimate=cost(3_000_000, 12_000_000),
        )(near, far, control, velocity, gradient)
    )


def solution(mesh):
    placed = (
        P(("window", "member"), "tile", None),
        P(("window", "member"), "tile", None),
        P(("window", "member"), None, "tile", None),
        P(("window", "member"), None, "tile", None),
        P("window", "tile"),
        P(),
        P(),
        P(),
    )
    return jax.shard_map(
        body,
        mesh=mesh,
        in_specs=placed,
        out_specs=(P(("window", "member"), "tile", None), P(("window", "member"), "tile", None)),
        check_vma=False,
    )
```

```python
import functools

import jax
import jax.numpy as jnp
from jax import lax
from jax.experimental import pallas as pl
from jax.experimental.pallas import tpu as pltpu
from jax.sharding import PartitionSpec as P

NZ = 64
SLOTS = 3
LANES = 128
EDGE = 3
F32 = jnp.float32
BF16 = jnp.bfloat16

VMEM = pl.BlockSpec(memory_space=pltpu.VMEM)
SMEM = pl.BlockSpec(memory_space=pltpu.SMEM)
HBM = pl.BlockSpec(memory_space=pltpu.HBM)


def params(mib):
    return pltpu.CompilerParams(vmem_limit_bytes=mib * 1024 * 1024)


def cost(flops, nbytes):
    return pl.CostEstimate(flops=flops, bytes_accessed=nbytes, transcendentals=0)


def in_hbm(array):
    return pltpu.with_memory_space_constraint(array, pltpu.HBM)


def split(value):
    high = value.astype(BF16)
    return high, (value - high.astype(F32)).astype(BF16)


def build_mix(mix, out_ref):
    zero = jnp.zeros((NZ, NZ), F32)
    pair = jnp.concatenate(
        [jnp.concatenate([mix, zero], axis=1), jnp.concatenate([zero, mix], axis=1)], axis=0
    )
    high, low = split(pair)
    out_ref[0:LANES, 0:LANES] = high
    out_ref[LANES:, 0:LANES] = high
    out_ref[0:LANES, LANES:] = low
    out_ref[LANES:, LANES:] = jnp.zeros((LANES, LANES), BF16)


def columns(tiles, taps):
    count = len(tiles)
    lower = lax.broadcasted_iota(jnp.int32, tiles[0].shape, 1) < NZ
    zero = jnp.zeros_like(tiles[0])
    turned = [pltpu.roll(tile, NZ, 1) for tile in tiles]
    between = {}
    for t in range(-1, count):
        first = turned[t] if t >= 0 else zero
        second = turned[t + 1] if t + 1 < count else zero
        between[t] = jnp.where(lower, first, second)
    outs = []
    for t in range(count):
        total = taps[3] * tiles[t]
        for k, at in ((1, t - 1), (5, t + 1)):
            if 0 <= at < count:
                total += taps[k] * tiles[at]
        for k, at in ((0, t - 2), (2, t - 1), (4, t), (6, t + 1)):
            if at in between:
                total += taps[k] * between[at]
        outs.append(total)
    return outs


def store_split(ref, stride, row, upper, lower):
    for t, (first, second) in enumerate(zip(upper, lower)):
        high, low = split(jnp.concatenate([first, second], axis=0))
        ref[stride * t + row : stride * t + row + 16, 0:LANES] = high
        ref[stride * t + row : stride * t + row + 16, LANES:] = low


def mixed(ref, start, size, matrix):
    both = jnp.dot(ref[start : start + size, :], matrix, preferred_element_type=F32)
    return both[:, 0:LANES] + both[:, LANES:]


def lanes_of(t):
    return slice(LANES * t, LANES * (t + 1))


def border_levels(rows_of, count, plain, lead, taps_y, left, matrix, result):
    sublane = lax.broadcasted_iota(jnp.int32, (8, LANES), 0)
    blocks = []
    for side in range(2):
        for row in range(0, 32, 8):
            place = lax.rem(sublane + row, EDGE)
            if side == 0:
                factors = [jnp.where(place < EDGE - d, plain[d], 0.0) for d in range(EDGE)]
            else:
                factors = [jnp.where(place >= d, lead[d], 0.0) for d in range(EDGE)]
            block = []
            for t in range(count):
                total = None
                for d in range(EDGE):
                    at = row + d if side == 0 else 8 + row - d
                    term = factors[d] * rows_of[side, t, at : at + 8, :]
                    total = term if total is None else total + term
                block.append(total)
            blocks.append(columns(block, taps_y))
            if len(blocks) == 2:
                store_split(left, 64, 32 * side + row - 8, *blocks)
                blocks = []
    group = 4
    for first in range(0, count, group):
        result[64 * first : 64 * (first + group), :] = mixed(left, 64 * first, 64 * group, matrix)


def clear_packed(rows_of, count):
    zero = jnp.zeros((8, LANES), F32)
    for t in range(count):
        rows_of[0, t, 24:32, :] = zero
        rows_of[0, t, 32:40, :] = zero
        rows_of[1, t, 0:8, :] = zero
        rows_of[1, t, 32:40, :] = zero


def stage_kernel(
    perturb_hbm, mine_hbm, mix_hbm, owner_hbm, taps_x_hbm, taps_y_hbm,
    perturb_ref, mine_ref, border_ref, matrix_ref, matrix_t_ref, vector_ref,
    mix, owner, taps_x, taps_y, sems,
):
    members, _, rows, cells = perturb_ref.shape
    small = ((mix_hbm, mix), (owner_hbm, owner), (taps_x_hbm, taps_x), (taps_y_hbm, taps_y))
    small = [pltpu.make_async_copy(src, dst, sems.at[members + 1 + i]) for i, (src, dst) in enumerate(small)]
    for copy in small:
        copy.start()
    copies = []
    for member in range(members):
        copies.append(pltpu.make_async_copy(perturb_hbm.at[member], perturb_ref.at[member], sems.at[member]))
    copies.append(pltpu.make_async_copy(mine_hbm, mine_ref, sems.at[members]))
    for copy in copies:
        copy.start()
    for copy in small:
        copy.wait()
    me = lax.axis_index("member")
    for slot in range(SLOTS):
        vector_ref[slot] = jnp.full((8, LANES), jnp.where(owner[slot] == me, 1.0, 0.0), F32)
    for k in range(7):
        vector_ref[SLOTS + k] = jnp.full((8, LANES), taps_x[k], F32)
        vector_ref[SLOTS + 7 + k] = jnp.full((8, LANES), taps_y[k], F32)
    build_mix(mix[...], matrix_ref)
    build_mix(mix[...].T, matrix_t_ref)
    for member in range(members):
        copies[member].wait()
        for slot in range(SLOTS):
            for t in range(cells // LANES):
                at = EDGE * (members * t + member)
                for side, start, first in ((0, 0, 0), (1, rows - 8, 8 - EDGE)):
                    value = perturb_ref[member, slot, start : start + 8, lanes_of(t)].astype(F32)
                    border_ref[slot, side, at : at + EDGE, :] = value[first : first + EDGE]
    copies[members].wait()


def by_parity(run, first, second):
    odd = lax.rem(lax.axis_index("tile"), 2) == 1
    pl.when(jnp.logical_not(odd))(lambda: run(first, second))
    pl.when(odd)(lambda: run(second, first))


def border_kernel(which, vector_ref, border_ref, mine_ref, other_ref, *refs):
    run = functools.partial(border_rows, vector_ref, border_ref, mine_ref, other_ref, refs[-1])
    odd = lax.rem(lax.axis_index("tile"), 2) == 1
    pl.when(jnp.logical_not(odd))(lambda: run(1 - which))
    pl.when(odd)(lambda: run(which))


def border_rows(vector_ref, border_ref, mine_ref, other_ref, out_ref, side):
    _, _, rows, cells = mine_ref.shape
    start = side * (rows - EDGE)
    total_rows = out_ref.shape[0]
    per_tile = total_rows // (cells // LANES)
    valid = [vector_ref[slot, 0:1, :] > 0.5 for slot in range(SLOTS)]
    sublane = lax.broadcasted_iota(jnp.int32, (8, LANES), 0)
    phase = [lax.rem(sublane + shift, EDGE) for shift in range(EDGE)]
    is_zero = [value == 0 for value in phase]
    is_one = [value == 1 for value in phase]
    whole = {}
    for t in range(cells // LANES):
        for slot in range(SLOTS):
            lines = []
            for i in range(EDGE):
                here = mine_ref[0, slot, start + i : start + i + 1, lanes_of(t)]
                there = other_ref[0, slot, start + i : start + i + 1, lanes_of(t)]
                lines.append(jnp.broadcast_to(jnp.where(valid[slot], here, there), (8, LANES)))
            for shift in range(EDGE):
                whole[t, slot, shift] = jnp.where(
                    is_zero[shift], lines[0], jnp.where(is_one[shift], lines[1], lines[2])
                )
        for row in range(0, total_rows, 8):
            if (row + 7) // per_tile != t:
                continue
            total = None
            for slot in range(SLOTS):
                field = whole[t, slot, row % EDGE]
                if row // per_tile != t:
                    field = jnp.where(sublane < per_tile * t - row, whole[t - 1, slot, row % EDGE], field)
                term = border_ref[slot, side, row : row + 8, :] * field
                total = term if total is None else total + term
            out_ref[row : row + 8, :] = total


def bulk_kernel(
    owner_ref, taps_x_ref, taps_y_ref, matrix, matrix_t, perturb_ref, mine_ref, other_ref, pair_ref, next_ref,
    control_hbm, velocity_hbm,
    local_ref, cross_pair_ref, cross_next_ref, square_ref, control_ref, velocity_ref,
    field, rows_of, packed, left, result, sems,
):
    members, _, rows, cells = perturb_ref.shape
    count = cells // LANES
    here = EDGE * members
    control_copy = pltpu.make_async_copy(control_hbm, control_ref, sems.at[0])
    velocity_copy = pltpu.make_async_copy(velocity_hbm, velocity_ref, sems.at[1])
    control_copy.start()
    velocity_copy.start()
    me = lax.axis_index("member")
    tile = lax.axis_index("tile")
    tiles = lax.axis_size("tile")
    taps_x = [taps_x_ref[k] for k in range(7)]
    taps_y = [taps_y_ref[k] for k in range(7)]
    first_taps, last_taps = taps_x[0:EDGE], taps_x[6 : 6 - EDGE : -1]
    for slot in range(SLOTS):
        field[slot] = jnp.where(owner_ref[slot] == me, mine_ref[0, slot], other_ref[0, slot])
    for half in range(2):
        rows_of[half, :, 0:8, :] = jnp.zeros((count, 8, LANES), F32)
        rows_of[half, :, rows + 8 : rows + 16, :] = jnp.zeros((count, 8, LANES), F32)
    clear_packed(packed, count)

    def unpack(up_ref, down_ref):
        for t in range(count):
            packed[0, t, 0:here, :] = up_ref[here * t : here * (t + 1), :]
            packed[1, t, 8 : 8 + here, :] = down_ref[here * t : here * (t + 1), :]

    by_parity(unpack, pair_ref, next_ref)
    border_levels(packed, count, first_taps, last_taps, taps_y, left, matrix[...], result)
    weights = [jnp.where(tile < tiles - 1, 1.0, 0.0).astype(F32), jnp.where(tile > 0, 1.0, 0.0).astype(F32)]
    squares = jnp.zeros((8, LANES), F32)
    for side in range(2):
        total = [jnp.zeros((8, LANES), F32) for _ in range(4)]
        for t in range(count):
            for step in range(4):
                value = result[64 * t + 32 * side + 8 * step : 64 * t + 32 * side + 8 * step + 8, :]
                total[step] += value * value
        squares += weights[side] * ((total[0] + total[1]) + (total[2] + total[3]))

    def pair_step(pair, carry):
        for half in range(2):
            member = 2 * pair + half
            for t in range(count):
                product = perturb_ref[member, 0, :, lanes_of(t)].astype(F32) * field[0, :, lanes_of(t)]
                for slot in range(1, SLOTS):
                    product += perturb_ref[member, slot, :, lanes_of(t)].astype(F32) * field[slot, :, lanes_of(t)]
                rows_of[half, t, 8 : 8 + rows, :] = product
        blocks = []
        size = 2 * rows
        for half in range(2):
            for row in range(0, rows, 8):
                block = []
                for t in range(count):
                    total = None
                    for k in range(7):
                        term = taps_x[k] * rows_of[half, t, row + k + 5 : row + k + 13, :]
                        total = term if total is None else total + term
                    block.append(total)
                blocks.append(columns(block, taps_y))
                if len(blocks) == 2:
                    store_split(left, size, half * rows + row - 8, *blocks)
                    blocks = []
        pl.when(pair == 0)(control_copy.wait)
        group = 4
        for first in range(0, count, group):
            out = mixed(left, size * first, size * group, matrix[...])
            for t in range(first, first + group):
                for half in range(2):
                    member = 2 * pair + half
                    base = size * (t - first) + rows * half
                    value = control_ref[member, :, lanes_of(t)] + out[base : base + rows]
                    local_ref[member, :, lanes_of(t)] = value
                    squared = value * value
                    for row in range(0, rows, 8):
                        carry += squared[row : row + 8]
                    packed[0, t, pl.ds(EDGE * member, EDGE), :] = value[rows - EDGE : rows]
                    packed[1, t, pl.ds(8 + EDGE * member, EDGE), :] = value[0:EDGE]
        return carry

    square_ref[...] = lax.fori_loop(0, members // 2, pair_step, squares)
    velocity_copy.wait()
    border_levels(packed, count, last_taps, first_taps, taps_y[::-1], left, matrix_t[...], result)

    def pack(cross_down_ref, cross_up_ref):
        for t in range(count):
            cross_down_ref[here * t : here * (t + 1), :] = result[64 * t : 64 * t + here, :]
            cross_up_ref[here * t : here * (t + 1), :] = result[64 * t + 32 : 64 * t + 32 + here, :]

    by_parity(pack, cross_pair_ref, cross_next_ref)


def cross_kernel(square_ref, cross_pair_ref, cross_next_ref, from_pair_ref, from_next_ref, total_ref):
    total = [jnp.zeros((8, LANES), F32) for _ in range(4)]
    for step, row in enumerate(range(0, cross_pair_ref.shape[0], 8)):
        at = slice(row, row + 8)
        which = 2 * (step % 2)
        total[which] += cross_pair_ref[at] * from_pair_ref[at]
        total[which + 1] += cross_next_ref[at] * from_next_ref[at]
    total_ref[...] = square_ref[...] + 2.0 * ((total[0] + total[1]) + (total[2] + total[3]))


def correct_kernel(
    vector_ref, matrix, from_pair_ref, from_next_ref, local_ref, gradient_ref, packed, left, result
):
    members, rows, cells = local_ref.shape
    count = cells // LANES
    here = EDGE * members
    taps_x = [vector_ref[SLOTS + k] for k in range(7)]
    taps_y = [vector_ref[SLOTS + 7 + k] for k in range(7)]
    clear_packed(packed, count)

    def unpack(from_right_ref, from_left_ref):
        for t in range(count):
            packed[0, t, 0:here, :] = from_left_ref[here * t : here * (t + 1), :]
            packed[1, t, 8 : 8 + here, :] = from_right_ref[here * t : here * (t + 1), :]

    by_parity(unpack, from_pair_ref, from_next_ref)
    border_levels(
        packed, count, taps_x[0:EDGE], taps_x[6 : 6 - EDGE : -1], taps_y, left, matrix[...], result
    )
    for member in range(members):
        for t in range(count):
            at = 64 * t + EDGE * member
            gradient_ref[member, 0:EDGE, lanes_of(t)] += result[at : at + EDGE, :]
            gradient_ref[member, rows - EDGE : rows, lanes_of(t)] += result[at + 32 : at + 32 + EDGE, :]


def update_kernel(
    entries, near_ref, far_ref, control_ref, velocity_ref, gradient_ref,
    new_control_hbm, new_velocity_hbm, new_control, new_velocity, sems,
):
    members, rows, cells = control_ref.shape
    mean = jnp.sum(near_ref[...] + far_ref[...], keepdims=True) / entries
    scale = lax.rsqrt(mean + 1e-06)
    copies = []
    for member in range(members):
        for start in range(0, rows, 8):
            tile = slice(start, start + 8)
            moved = 0.9 * velocity_ref[member, tile] + scale * gradient_ref[member, tile]
            new_velocity[member, tile] = moved
            new_control[member, tile] = control_ref[member, tile] - 0.5 * moved
        for which, (src, dst) in enumerate(((new_control, new_control_hbm), (new_velocity, new_velocity_hbm))):
            copy = pltpu.make_async_copy(src.at[member], dst.at[member], sems.at[which, member])
            copy.start()
            copies.append(copy)
    for copy in copies:
        copy.wait()


def body(control, velocity, perturb, adjoint_forcing, slot_owner, taps_x, taps_y, vertical_mix):
    members, rows, cells = control.shape
    count = cells // LANES
    tiles = lax.axis_size("tile")
    groups = lax.axis_size("member")
    owner = slot_owner.reshape(SLOTS)
    swap = [(0, 1), (1, 0)]
    other = lax.ppermute(adjoint_forcing, "member", swap)
    edges = EDGE * members * count
    square_matrix = (2 * LANES, 2 * LANES)
    perturb, mine, border, matrix, matrix_t, vectors = pl.pallas_call(
        stage_kernel,
        name="stage",
        out_shape=(
            jax.ShapeDtypeStruct(perturb.shape, perturb.dtype),
            jax.ShapeDtypeStruct(adjoint_forcing.shape, F32),
            jax.ShapeDtypeStruct((SLOTS, 2, edges, LANES), F32),
            jax.ShapeDtypeStruct(square_matrix, BF16),
            jax.ShapeDtypeStruct(square_matrix, BF16),
            jax.ShapeDtypeStruct((SLOTS + 14, 8, LANES), F32),
        ),
        in_specs=[HBM] * 6,
        out_specs=(VMEM,) * 6,
        scratch_shapes=[
            pltpu.VMEM(vertical_mix.shape, F32),
            pltpu.SMEM((SLOTS,), jnp.int32),
            pltpu.SMEM((7,), F32),
            pltpu.SMEM((7,), F32),
            pltpu.SemaphoreType.DMA((members + 5,)),
        ],
        compiler_params=params(8),
        cost_estimate=cost(0, 8_000_000),
    )(*map(in_hbm, (perturb, adjoint_forcing, vertical_mix, owner, taps_x, taps_y)))
    packed = jax.ShapeDtypeStruct((edges, LANES), F32)
    sent = []
    for which in range(2):
        sent.append(
            pl.pallas_call(
                functools.partial(border_kernel, which),
                name=f"border_product_{which}",
                out_shape=packed,
                in_specs=[VMEM, VMEM, VMEM, VMEM] + [pl.BlockSpec(memory_space=pl.ANY)] * which,
                out_specs=VMEM,
                compiler_params=params(8),
                cost_estimate=cost(2_000_000, 2_000_000),
            )(vectors, border, mine, other, *sent)
        )
    pair, after = sent
    swaps = [(i, i + 1) for i in range(tiles - 1)] + [(i + 1, i) for i in range(tiles - 1)]
    from_next = lax.ppermute(after, "tile", [(i, j) for i, j in swaps if min(i, j) % 2 == 1])
    from_pair = lax.ppermute(pair, "tile", [(i, j) for i, j in swaps if min(i, j) % 2 == 0])
    border_scratch = [
        pltpu.VMEM((2, count, 40, LANES), F32),
        pltpu.VMEM((count * 64, 2 * LANES), BF16),
        pltpu.VMEM((count * 64, LANES), F32),
    ]
    whole = jax.ShapeDtypeStruct(control.shape, F32)
    local, cross_pair, cross_next, square, control, velocity = pl.pallas_call(
        bulk_kernel,
        name="bulk",
        out_shape=(whole, packed, packed, jax.ShapeDtypeStruct((8, LANES), F32), whole, whole),
        in_specs=[SMEM, SMEM, SMEM] + [VMEM] * 7 + [HBM, HBM],
        out_specs=(VMEM,) * 6,
        scratch_shapes=[
            pltpu.VMEM((SLOTS, rows, cells), F32),
            pltpu.VMEM((2, count, rows + 16, LANES), F32),
            *border_scratch,
            pltpu.SemaphoreType.DMA((2,)),
        ],
        compiler_params=params(24),
        cost_estimate=cost(9_000_000_000, 12_000_000),
    )(
        owner, taps_x, taps_y, matrix, matrix_t, perturb, mine, other, pair, after,
        in_hbm(control), in_hbm(velocity),
    )
    near = pl.pallas_call(
        cross_kernel,
        name="cross_term",
        out_shape=jax.ShapeDtypeStruct((8, LANES), F32),
        in_specs=[VMEM] * 5,
        out_specs=VMEM,
        compiler_params=params(8),
        cost_estimate=cost(200_000, 1_000_000),
    )(square, cross_pair, cross_next, from_pair, from_next)
    gradient = pl.pallas_call(
        correct_kernel,
        name="border_correction",
        out_shape=whole,
        in_specs=[VMEM] * 5,
        out_specs=VMEM,
        scratch_shapes=border_scratch,
        input_output_aliases={4: 0},
        compiler_params=params(16),
        cost_estimate=cost(2_000_000_000, 2_000_000),
    )(vectors, matrix, from_pair, from_next, local)
    near = near + lax.ppermute(near, "member", swap)
    steps = []
    width = 1
    while width < tiles:
        steps.append([(groups * i + g, groups * (i ^ width) + groups - 1 - g) for i in range(tiles) for g in range(groups)])
        width *= 2
    for pairs in steps[:-1]:
        near = near + lax.ppermute(near, ("tile", "member"), pairs)
    far = lax.ppermute(near, ("tile", "member"), steps[-1])
    entries = members * groups * rows * tiles * cells
    return tuple(
        pl.pallas_call(
            functools.partial(update_kernel, float(entries)),
            name="update",
            out_shape=(whole, whole),
            in_specs=[VMEM] * 5,
            out_specs=(HBM, HBM),
            scratch_shapes=[
                pltpu.VMEM(control.shape, F32),
                pltpu.VMEM(control.shape, F32),
                pltpu.SemaphoreType.DMA((2, members)),
            ],
            compiler_params=params(16),
            cost_estimate=cost(3_000_000, 12_000_000),
        )(near, far, control, velocity, gradient)
    )


def solution(mesh):
    placed = (
        P(("window", "member"), "tile", None),
        P(("window", "member"), "tile", None),
        P(("window", "member"), None, "tile", None),
        P(("window", "member"), None, "tile", None),
        P("window", "tile"),
        P(),
        P(),
        P(),
    )
    return jax.shard_map(
        body,
        mesh=mesh,
        in_specs=placed,
        out_specs=(P(("window", "member"), "tile", None), P(("window", "member"), "tile", None)),
        check_vma=False,
    )
```

```python
import functools

import jax
import jax.numpy as jnp
from jax import lax
from jax.experimental import pallas as pl
from jax.experimental.pallas import tpu as pltpu
from jax.sharding import PartitionSpec as P

NZ = 64
SLOTS = 3
LANES = 128
EDGE = 3
F32 = jnp.float32
BF16 = jnp.bfloat16

VMEM = pl.BlockSpec(memory_space=pltpu.VMEM)
SMEM = pl.BlockSpec(memory_space=pltpu.SMEM)
HBM = pl.BlockSpec(memory_space=pltpu.HBM)


def params(mib):
    return pltpu.CompilerParams(vmem_limit_bytes=mib * 1024 * 1024)


def cost(flops, nbytes):
    return pl.CostEstimate(flops=flops, bytes_accessed=nbytes, transcendentals=0)


def in_hbm(array):
    return pltpu.with_memory_space_constraint(array, pltpu.HBM)


def split(value):
    high = value.astype(BF16)
    return high, (value - high.astype(F32)).astype(BF16)


def build_mix(mix, out_ref):
    zero = jnp.zeros((NZ, NZ), F32)
    pair = jnp.concatenate(
        [jnp.concatenate([mix, zero], axis=1), jnp.concatenate([zero, mix], axis=1)], axis=0
    )
    high, low = split(pair)
    out_ref[0:LANES, 0:LANES] = high
    out_ref[LANES:, 0:LANES] = high
    out_ref[0:LANES, LANES:] = low
    out_ref[LANES:, LANES:] = jnp.zeros((LANES, LANES), BF16)


def columns(tiles, taps):
    count = len(tiles)
    lower = lax.broadcasted_iota(jnp.int32, tiles[0].shape, 1) < NZ
    zero = jnp.zeros_like(tiles[0])
    turned = [pltpu.roll(tile, NZ, 1) for tile in tiles]
    between = {}
    for t in range(-1, count):
        first = turned[t] if t >= 0 else zero
        second = turned[t + 1] if t + 1 < count else zero
        between[t] = jnp.where(lower, first, second)
    outs = []
    for t in range(count):
        total = taps[3] * tiles[t]
        for k, at in ((1, t - 1), (5, t + 1)):
            if 0 <= at < count:
                total += taps[k] * tiles[at]
        for k, at in ((0, t - 2), (2, t - 1), (4, t), (6, t + 1)):
            if at in between:
                total += taps[k] * between[at]
        outs.append(total)
    return outs


def store_split(ref, stride, row, upper, lower):
    for t, (first, second) in enumerate(zip(upper, lower)):
        high, low = split(jnp.concatenate([first, second], axis=0))
        ref[stride * t + row : stride * t + row + 16, 0:LANES] = high
        ref[stride * t + row : stride * t + row + 16, LANES:] = low


def mixed(ref, start, size, matrix):
    both = jnp.dot(ref[start : start + size, :], matrix, preferred_element_type=F32)
    return both[:, 0:LANES] + both[:, LANES:]


def lanes_of(t):
    return slice(LANES * t, LANES * (t + 1))


def border_levels(rows_of, count, plain, lead, taps_y, left, matrix, result):
    sublane = lax.broadcasted_iota(jnp.int32, (8, LANES), 0)
    blocks = []
    for side in range(2):
        for row in range(0, 32, 8):
            place = lax.rem(sublane + row, EDGE)
            if side == 0:
                factors = [jnp.where(place < EDGE - d, plain[d], 0.0) for d in range(EDGE)]
            else:
                factors = [jnp.where(place >= d, lead[d], 0.0) for d in range(EDGE)]
            block = []
            for t in range(count):
                total = None
                for d in range(EDGE):
                    at = row + d if side == 0 else 8 + row - d
                    term = factors[d] * rows_of[side, t, at : at + 8, :]
                    total = term if total is None else total + term
                block.append(total)
            blocks.append(columns(block, taps_y))
            if len(blocks) == 2:
                store_split(left, 64, 32 * side + row - 8, *blocks)
                blocks = []
    group = 4
    for first in range(0, count, group):
        result[64 * first : 64 * (first + group), :] = mixed(left, 64 * first, 64 * group, matrix)


def clear_packed(rows_of, count):
    zero = jnp.zeros((8, LANES), F32)
    for t in range(count):
        rows_of[0, t, 24:32, :] = zero
        rows_of[0, t, 32:40, :] = zero
        rows_of[1, t, 0:8, :] = zero
        rows_of[1, t, 32:40, :] = zero


def stage_kernel(
    perturb_hbm, mine_hbm, mix_hbm, owner_hbm, taps_x_hbm, taps_y_hbm,
    perturb_ref, mine_ref, border_ref, matrix_ref, matrix_t_ref, vector_ref,
    mix, owner, taps_x, taps_y, sems,
):
    members, _, rows, cells = perturb_ref.shape
    small = ((mix_hbm, mix), (owner_hbm, owner), (taps_x_hbm, taps_x), (taps_y_hbm, taps_y))
    small = [pltpu.make_async_copy(src, dst, sems.at[members + 1 + i]) for i, (src, dst) in enumerate(small)]
    for copy in small:
        copy.start()
    copies = []
    for member in range(members):
        copies.append(pltpu.make_async_copy(perturb_hbm.at[member], perturb_ref.at[member], sems.at[member]))
    copies.append(pltpu.make_async_copy(mine_hbm, mine_ref, sems.at[members]))
    for copy in copies:
        copy.start()
    for copy in small:
        copy.wait()
    me = lax.axis_index("member")
    for slot in range(SLOTS):
        vector_ref[slot] = jnp.full((8, LANES), jnp.where(owner[slot] == me, 1.0, 0.0), F32)
    for k in range(7):
        vector_ref[SLOTS + k] = jnp.full((8, LANES), taps_x[k], F32)
        vector_ref[SLOTS + 7 + k] = jnp.full((8, LANES), taps_y[k], F32)
    build_mix(mix[...], matrix_ref)
    build_mix(mix[...].T, matrix_t_ref)
    for member in range(members):
        copies[member].wait()
        for slot in range(SLOTS):
            for t in range(cells // LANES):
                at = EDGE * (members * t + member)
                for side, start, first in ((0, 0, 0), (1, rows - 8, 8 - EDGE)):
                    value = perturb_ref[member, slot, start : start + 8, lanes_of(t)].astype(F32)
                    border_ref[slot, side, at : at + EDGE, :] = value[first : first + EDGE]
    copies[members].wait()


def by_parity(run, first, second):
    odd = lax.rem(lax.axis_index("tile"), 2) == 1
    pl.when(jnp.logical_not(odd))(lambda: run(first, second))
    pl.when(odd)(lambda: run(second, first))


def border_kernel(which, vector_ref, border_ref, mine_ref, other_ref, *refs):
    run = functools.partial(border_rows, vector_ref, border_ref, mine_ref, other_ref, refs[-1])
    odd = lax.rem(lax.axis_index("tile"), 2) == 1
    pl.when(jnp.logical_not(odd))(lambda: run(1 - which))
    pl.when(odd)(lambda: run(which))


def border_rows(vector_ref, border_ref, mine_ref, other_ref, out_ref, side):
    _, _, rows, cells = mine_ref.shape
    start = side * (rows - EDGE)
    total_rows = out_ref.shape[0]
    per_tile = total_rows // (cells // LANES)
    valid = [vector_ref[slot, 0:1, :] > 0.5 for slot in range(SLOTS)]
    sublane = lax.broadcasted_iota(jnp.int32, (8, LANES), 0)
    phase = [lax.rem(sublane + shift, EDGE) for shift in range(EDGE)]
    is_zero = [value == 0 for value in phase]
    is_one = [value == 1 for value in phase]
    whole = {}
    for t in range(cells // LANES):
        for slot in range(SLOTS):
            lines = []
            for i in range(EDGE):
                here = mine_ref[0, slot, start + i : start + i + 1, lanes_of(t)]
                there = other_ref[0, slot, start + i : start + i + 1, lanes_of(t)]
                lines.append(jnp.broadcast_to(jnp.where(valid[slot], here, there), (8, LANES)))
            for shift in range(EDGE):
                whole[t, slot, shift] = jnp.where(
                    is_zero[shift], lines[0], jnp.where(is_one[shift], lines[1], lines[2])
                )
        for row in range(0, total_rows, 8):
            if (row + 7) // per_tile != t:
                continue
            total = None
            for slot in range(SLOTS):
                field = whole[t, slot, row % EDGE]
                if row // per_tile != t:
                    field = jnp.where(sublane < per_tile * t - row, whole[t - 1, slot, row % EDGE], field)
                term = border_ref[slot, side, row : row + 8, :] * field
                total = term if total is None else total + term
            out_ref[row : row + 8, :] = total


def bulk_kernel(
    owner_ref, taps_x_ref, taps_y_ref, matrix, matrix_t, perturb_ref, mine_ref, other_ref, pair_ref, next_ref,
    control_hbm, velocity_hbm,
    local_ref, cross_pair_ref, cross_next_ref, square_ref, control_ref, velocity_ref,
    field, rows_of, packed, left, result, sems,
):
    members, _, rows, cells = perturb_ref.shape
    count = cells // LANES
    here = EDGE * members
    control_copy = pltpu.make_async_copy(control_hbm, control_ref, sems.at[0])
    velocity_copy = pltpu.make_async_copy(velocity_hbm, velocity_ref, sems.at[1])
    control_copy.start()
    velocity_copy.start()
    me = lax.axis_index("member")
    tile = lax.axis_index("tile")
    tiles = lax.axis_size("tile")
    taps_x = [taps_x_ref[k] for k in range(7)]
    taps_y = [taps_y_ref[k] for k in range(7)]
    first_taps, last_taps = taps_x[0:EDGE], taps_x[6 : 6 - EDGE : -1]
    for slot in range(SLOTS):
        field[slot] = jnp.where(owner_ref[slot] == me, mine_ref[0, slot], other_ref[0, slot])
    for half in range(2):
        rows_of[half, :, 0:8, :] = jnp.zeros((count, 8, LANES), F32)
        rows_of[half, :, rows + 8 : rows + 16, :] = jnp.zeros((count, 8, LANES), F32)
    clear_packed(packed, count)

    def unpack(up_ref, down_ref):
        for t in range(count):
            packed[0, t, 0:here, :] = up_ref[here * t : here * (t + 1), :]
            packed[1, t, 8 : 8 + here, :] = down_ref[here * t : here * (t + 1), :]

    by_parity(unpack, pair_ref, next_ref)
    border_levels(packed, count, first_taps, last_taps, taps_y, left, matrix[...], result)
    weights = [jnp.where(tile < tiles - 1, 1.0, 0.0).astype(F32), jnp.where(tile > 0, 1.0, 0.0).astype(F32)]
    squares = jnp.zeros((8, LANES), F32)
    for side in range(2):
        total = [jnp.zeros((8, LANES), F32) for _ in range(4)]
        for t in range(count):
            for step in range(4):
                value = result[64 * t + 32 * side + 8 * step : 64 * t + 32 * side + 8 * step + 8, :]
                total[step] += value * value
        squares += weights[side] * ((total[0] + total[1]) + (total[2] + total[3]))

    def pair_step(pair, carry):
        for half in range(2):
            member = 2 * pair + half
            for t in range(count):
                product = perturb_ref[member, 0, :, lanes_of(t)].astype(F32) * field[0, :, lanes_of(t)]
                for slot in range(1, SLOTS):
                    product += perturb_ref[member, slot, :, lanes_of(t)].astype(F32) * field[slot, :, lanes_of(t)]
                rows_of[half, t, 8 : 8 + rows, :] = product
        blocks = []
        size = 2 * rows
        for half in range(2):
            for row in range(0, rows, 8):
                block = []
                for t in range(count):
                    total = None
                    for k in range(7):
                        term = taps_x[k] * rows_of[half, t, row + k + 5 : row + k + 13, :]
                        total = term if total is None else total + term
                    block.append(total)
                blocks.append(columns(block, taps_y))
                if len(blocks) == 2:
                    store_split(left, size, half * rows + row - 8, *blocks)
                    blocks = []
        pl.when(pair == 0)(control_copy.wait)
        group = 4
        for first in range(0, count, group):
            out = mixed(left, size * first, size * group, matrix[...])
            for t in range(first, first + group):
                for half in range(2):
                    member = 2 * pair + half
                    base = size * (t - first) + rows * half
                    value = control_ref[member, :, lanes_of(t)] + out[base : base + rows]
                    local_ref[member, :, lanes_of(t)] = value
                    squared = value * value
                    for row in range(0, rows, 8):
                        carry += squared[row : row + 8]
                    packed[0, t, pl.ds(EDGE * member, EDGE), :] = value[rows - EDGE : rows]
                    packed[1, t, pl.ds(8 + EDGE * member, EDGE), :] = value[0:EDGE]
        return carry

    square_ref[...] = lax.fori_loop(0, members // 2, pair_step, squares)
    velocity_copy.wait()
    border_levels(packed, count, last_taps, first_taps, taps_y[::-1], left, matrix_t[...], result)

    def pack(cross_down_ref, cross_up_ref):
        for t in range(count):
            cross_down_ref[here * t : here * (t + 1), :] = result[64 * t : 64 * t + here, :]
            cross_up_ref[here * t : here * (t + 1), :] = result[64 * t + 32 : 64 * t + 32 + here, :]

    by_parity(pack, cross_pair_ref, cross_next_ref)


def cross_kernel(square_ref, cross_pair_ref, cross_next_ref, from_pair_ref, from_next_ref, total_ref):
    total = [jnp.zeros((8, LANES), F32) for _ in range(4)]
    for step, row in enumerate(range(0, cross_pair_ref.shape[0], 8)):
        at = slice(row, row + 8)
        which = 2 * (step % 2)
        total[which] += cross_pair_ref[at] * from_pair_ref[at]
        total[which + 1] += cross_next_ref[at] * from_next_ref[at]
    whole = square_ref[...] + 2.0 * ((total[0] + total[1]) + (total[2] + total[3]))
    total_ref[...] = jnp.sum(whole, axis=0, keepdims=True)


def correct_kernel(
    vector_ref, matrix, from_pair_ref, from_next_ref, local_ref, gradient_ref, packed, left, result
):
    members, rows, cells = local_ref.shape
    count = cells // LANES
    here = EDGE * members
    taps_x = [vector_ref[SLOTS + k] for k in range(7)]
    taps_y = [vector_ref[SLOTS + 7 + k] for k in range(7)]
    clear_packed(packed, count)

    def unpack(from_right_ref, from_left_ref):
        for t in range(count):
            packed[0, t, 0:here, :] = from_left_ref[here * t : here * (t + 1), :]
            packed[1, t, 8 : 8 + here, :] = from_right_ref[here * t : here * (t + 1), :]

    by_parity(unpack, from_pair_ref, from_next_ref)
    border_levels(
        packed, count, taps_x[0:EDGE], taps_x[6 : 6 - EDGE : -1], taps_y, left, matrix[...], result
    )
    for member in range(members):
        for t in range(count):
            at = 64 * t + EDGE * member
            gradient_ref[member, 0:EDGE, lanes_of(t)] += result[at : at + EDGE, :]
            gradient_ref[member, rows - EDGE : rows, lanes_of(t)] += result[at + 32 : at + 32 + EDGE, :]


def update_kernel(
    entries, near_ref, far_ref, control_ref, velocity_ref, gradient_ref,
    new_control_hbm, new_velocity_hbm, new_control, new_velocity, sems,
):
    members, rows, cells = control_ref.shape
    mean = jnp.sum(near_ref[...] + far_ref[...], keepdims=True) / entries
    scale = lax.rsqrt(mean + 1e-06)
    copies = []
    for member in range(members):
        for start in range(0, rows, 8):
            tile = slice(start, start + 8)
            moved = 0.9 * velocity_ref[member, tile] + scale * gradient_ref[member, tile]
            new_velocity[member, tile] = moved
            new_control[member, tile] = control_ref[member, tile] - 0.5 * moved
        for which, (src, dst) in enumerate(((new_control, new_control_hbm), (new_velocity, new_velocity_hbm))):
            copy = pltpu.make_async_copy(src.at[member], dst.at[member], sems.at[which, member])
            copy.start()
            copies.append(copy)
    for copy in copies:
        copy.wait()


def body(control, velocity, perturb, adjoint_forcing, slot_owner, taps_x, taps_y, vertical_mix):
    members, rows, cells = control.shape
    count = cells // LANES
    tiles = lax.axis_size("tile")
    groups = lax.axis_size("member")
    owner = slot_owner.reshape(SLOTS)
    swap = [(0, 1), (1, 0)]
    other = lax.ppermute(adjoint_forcing, "member", swap)
    edges = EDGE * members * count
    square_matrix = (2 * LANES, 2 * LANES)
    perturb, mine, border, matrix, matrix_t, vectors = pl.pallas_call(
        stage_kernel,
        name="stage",
        out_shape=(
            jax.ShapeDtypeStruct(perturb.shape, perturb.dtype),
            jax.ShapeDtypeStruct(adjoint_forcing.shape, F32),
            jax.ShapeDtypeStruct((SLOTS, 2, edges, LANES), F32),
            jax.ShapeDtypeStruct(square_matrix, BF16),
            jax.ShapeDtypeStruct(square_matrix, BF16),
            jax.ShapeDtypeStruct((SLOTS + 14, 8, LANES), F32),
        ),
        in_specs=[HBM] * 6,
        out_specs=(VMEM,) * 6,
        scratch_shapes=[
            pltpu.VMEM(vertical_mix.shape, F32),
            pltpu.SMEM((SLOTS,), jnp.int32),
            pltpu.SMEM((7,), F32),
            pltpu.SMEM((7,), F32),
            pltpu.SemaphoreType.DMA((members + 5,)),
        ],
        compiler_params=params(8),
        cost_estimate=cost(0, 8_000_000),
    )(*map(in_hbm, (perturb, adjoint_forcing, vertical_mix, owner, taps_x, taps_y)))
    packed = jax.ShapeDtypeStruct((edges, LANES), F32)
    sent = []
    for which in range(2):
        sent.append(
            pl.pallas_call(
                functools.partial(border_kernel, which),
                name=f"border_product_{which}",
                out_shape=packed,
                in_specs=[VMEM, VMEM, VMEM, VMEM] + [pl.BlockSpec(memory_space=pl.ANY)] * which,
                out_specs=VMEM,
                compiler_params=params(8),
                cost_estimate=cost(2_000_000, 2_000_000),
            )(vectors, border, mine, other, *sent)
        )
    pair, after = sent
    swaps = [(i, i + 1) for i in range(tiles - 1)] + [(i + 1, i) for i in range(tiles - 1)]
    from_next = lax.ppermute(after, "tile", [(i, j) for i, j in swaps if min(i, j) % 2 == 1])
    from_pair = lax.ppermute(pair, "tile", [(i, j) for i, j in swaps if min(i, j) % 2 == 0])
    border_scratch = [
        pltpu.VMEM((2, count, 40, LANES), F32),
        pltpu.VMEM((count * 64, 2 * LANES), BF16),
        pltpu.VMEM((count * 64, LANES), F32),
    ]
    whole = jax.ShapeDtypeStruct(control.shape, F32)
    local, cross_pair, cross_next, square, control, velocity = pl.pallas_call(
        bulk_kernel,
        name="bulk",
        out_shape=(whole, packed, packed, jax.ShapeDtypeStruct((8, LANES), F32), whole, whole),
        in_specs=[SMEM, SMEM, SMEM] + [VMEM] * 7 + [HBM, HBM],
        out_specs=(VMEM,) * 6,
        scratch_shapes=[
            pltpu.VMEM((SLOTS, rows, cells), F32),
            pltpu.VMEM((2, count, rows + 16, LANES), F32),
            *border_scratch,
            pltpu.SemaphoreType.DMA((2,)),
        ],
        compiler_params=params(24),
        cost_estimate=cost(9_000_000_000, 12_000_000),
    )(
        owner, taps_x, taps_y, matrix, matrix_t, perturb, mine, other, pair, after,
        in_hbm(control), in_hbm(velocity),
    )
    near = pl.pallas_call(
        cross_kernel,
        name="cross_term",
        out_shape=jax.ShapeDtypeStruct((1, LANES), F32),
        in_specs=[VMEM] * 5,
        out_specs=VMEM,
        compiler_params=params(8),
        cost_estimate=cost(200_000, 1_000_000),
    )(square, cross_pair, cross_next, from_pair, from_next)
    gradient = pl.pallas_call(
        correct_kernel,
        name="border_correction",
        out_shape=whole,
        in_specs=[VMEM] * 5,
        out_specs=VMEM,
        scratch_shapes=border_scratch,
        input_output_aliases={4: 0},
        compiler_params=params(16),
        cost_estimate=cost(2_000_000_000, 2_000_000),
    )(vectors, matrix, from_pair, from_next, local)
    near = near + lax.ppermute(near, "member", swap)
    steps = []
    width = 1
    while width < tiles:
        steps.append([(groups * i + g, groups * (i ^ width) + groups - 1 - g) for i in range(tiles) for g in range(groups)])
        width *= 2
    for pairs in steps[:-1]:
        near = near + lax.ppermute(near, ("tile", "member"), pairs)
    far = lax.ppermute(near, ("tile", "member"), steps[-1])
    entries = members * groups * rows * tiles * cells
    return tuple(
        pl.pallas_call(
            functools.partial(update_kernel, float(entries)),
            name="update",
            out_shape=(whole, whole),
            in_specs=[VMEM] * 5,
            out_specs=(HBM, HBM),
            scratch_shapes=[
                pltpu.VMEM(control.shape, F32),
                pltpu.VMEM(control.shape, F32),
                pltpu.SemaphoreType.DMA((2, members)),
            ],
            compiler_params=params(16),
            cost_estimate=cost(3_000_000, 12_000_000),
        )(near, far, control, velocity, gradient)
    )


def solution(mesh):
    placed = (
        P(("window", "member"), "tile", None),
        P(("window", "member"), "tile", None),
        P(("window", "member"), None, "tile", None),
        P(("window", "member"), None, "tile", None),
        P("window", "tile"),
        P(),
        P(),
        P(),
    )
    return jax.shard_map(
        body,
        mesh=mesh,
        in_specs=placed,
        out_specs=(P(("window", "member"), "tile", None), P(("window", "member"), "tile", None)),
        check_vma=False,
    )
```

```python
import functools

import jax
import jax.numpy as jnp
from jax import lax
from jax.experimental import pallas as pl
from jax.experimental.pallas import tpu as pltpu
from jax.sharding import PartitionSpec as P

NZ = 64
SLOTS = 3
LANES = 128
EDGE = 3
F32 = jnp.float32
BF16 = jnp.bfloat16

VMEM = pl.BlockSpec(memory_space=pltpu.VMEM)
SMEM = pl.BlockSpec(memory_space=pltpu.SMEM)
HBM = pl.BlockSpec(memory_space=pltpu.HBM)


def params(mib):
    return pltpu.CompilerParams(vmem_limit_bytes=mib * 1024 * 1024)


def cost(flops, nbytes):
    return pl.CostEstimate(flops=flops, bytes_accessed=nbytes, transcendentals=0)


def in_hbm(array):
    return pltpu.with_memory_space_constraint(array, pltpu.HBM)


def split(value):
    high = value.astype(BF16)
    return high, (value - high.astype(F32)).astype(BF16)


def build_mix(mix, out_ref):
    zero = jnp.zeros((NZ, NZ), F32)
    pair = jnp.concatenate(
        [jnp.concatenate([mix, zero], axis=1), jnp.concatenate([zero, mix], axis=1)], axis=0
    )
    high, low = split(pair)
    out_ref[0:LANES, 0:LANES] = high
    out_ref[LANES:, 0:LANES] = high
    out_ref[0:LANES, LANES:] = low
    out_ref[LANES:, LANES:] = jnp.zeros((LANES, LANES), BF16)


def columns(tiles, taps):
    count = len(tiles)
    lower = lax.broadcasted_iota(jnp.int32, tiles[0].shape, 1) < NZ
    zero = jnp.zeros_like(tiles[0])
    turned = [pltpu.roll(tile, NZ, 1) for tile in tiles]
    between = {}
    for t in range(-1, count):
        first = turned[t] if t >= 0 else zero
        second = turned[t + 1] if t + 1 < count else zero
        between[t] = jnp.where(lower, first, second)
    outs = []
    for t in range(count):
        total = taps[3] * tiles[t]
        for k, at in ((1, t - 1), (5, t + 1)):
            if 0 <= at < count:
                total += taps[k] * tiles[at]
        for k, at in ((0, t - 2), (2, t - 1), (4, t), (6, t + 1)):
            if at in between:
                total += taps[k] * between[at]
        outs.append(total)
    return outs


def store_split(ref, stride, row, upper, lower):
    for t, (first, second) in enumerate(zip(upper, lower)):
        high, low = split(jnp.concatenate([first, second], axis=0))
        ref[stride * t + row : stride * t + row + 16, 0:LANES] = high
        ref[stride * t + row : stride * t + row + 16, LANES:] = low


def mixed(ref, start, size, matrix):
    both = jnp.dot(ref[start : start + size, :], matrix, preferred_element_type=F32)
    return both[:, 0:LANES] + both[:, LANES:]


def lanes_of(t):
    return slice(LANES * t, LANES * (t + 1))


def border_levels(rows_of, count, plain, lead, taps_y, left, matrix, result):
    sublane = lax.broadcasted_iota(jnp.int32, (8, LANES), 0)
    blocks = []
    for side in range(2):
        for row in range(0, 32, 8):
            place = lax.rem(sublane + row, EDGE)
            if side == 0:
                factors = [jnp.where(place < EDGE - d, plain[d], 0.0) for d in range(EDGE)]
            else:
                factors = [jnp.where(place >= d, lead[d], 0.0) for d in range(EDGE)]
            block = []
            for t in range(count):
                total = None
                for d in range(EDGE):
                    at = row + d if side == 0 else 8 + row - d
                    term = factors[d] * rows_of[side, t, at : at + 8, :]
                    total = term if total is None else total + term
                block.append(total)
            blocks.append(columns(block, taps_y))
            if len(blocks) == 2:
                store_split(left, 64, 32 * side + row - 8, *blocks)
                blocks = []
    group = 4
    for first in range(0, count, group):
        result[64 * first : 64 * (first + group), :] = mixed(left, 64 * first, 64 * group, matrix)


def clear_packed(rows_of, count):
    zero = jnp.zeros((8, LANES), F32)
    for t in range(count):
        rows_of[0, t, 24:32, :] = zero
        rows_of[0, t, 32:40, :] = zero
        rows_of[1, t, 0:8, :] = zero
        rows_of[1, t, 32:40, :] = zero


def stage_kernel(
    perturb_hbm, mine_hbm, mix_hbm, owner_hbm, taps_x_hbm, taps_y_hbm,
    perturb_ref, mine_ref, border_ref, matrix_ref, matrix_t_ref, vector_ref,
    mix, owner, taps_x, taps_y, sems,
):
    members, _, rows, cells = perturb_ref.shape
    small = ((mix_hbm, mix), (owner_hbm, owner), (taps_x_hbm, taps_x), (taps_y_hbm, taps_y))
    small = [pltpu.make_async_copy(src, dst, sems.at[members + 2 + i]) for i, (src, dst) in enumerate(small)]
    for copy in small:
        copy.start()
    copies = []
    for member in range(members):
        copies.append(pltpu.make_async_copy(perturb_hbm.at[member], perturb_ref.at[member], sems.at[member]))
    for side, start in enumerate((0, rows - 8)):
        source = mine_hbm.at[0, :, pl.ds(start, 8)]
        copies.append(pltpu.make_async_copy(source, mine_ref.at[side], sems.at[members + side]))
    for copy in copies:
        copy.start()
    for copy in small:
        copy.wait()
    me = lax.axis_index("member")
    for slot in range(SLOTS):
        vector_ref[slot] = jnp.full((8, LANES), jnp.where(owner[slot] == me, 1.0, 0.0), F32)
    for k in range(7):
        vector_ref[SLOTS + k] = jnp.full((8, LANES), taps_x[k], F32)
        vector_ref[SLOTS + 7 + k] = jnp.full((8, LANES), taps_y[k], F32)
    build_mix(mix[...], matrix_ref)
    build_mix(mix[...].T, matrix_t_ref)
    for member in range(members):
        copies[member].wait()
        for slot in range(SLOTS):
            for t in range(cells // LANES):
                at = EDGE * (members * t + member)
                for side, start, first in ((0, 0, 0), (1, rows - 8, 8 - EDGE)):
                    value = perturb_ref[member, slot, start : start + 8, lanes_of(t)].astype(F32)
                    border_ref[slot, side, at : at + EDGE, :] = value[first : first + EDGE]
    copies[members].wait()
    copies[members + 1].wait()


def by_parity(run, first, second):
    odd = lax.rem(lax.axis_index("tile"), 2) == 1
    pl.when(jnp.logical_not(odd))(lambda: run(first, second))
    pl.when(odd)(lambda: run(second, first))


def border_kernel(which, vector_ref, border_ref, mine_ref, other_ref, *refs):
    run = functools.partial(border_rows, vector_ref, border_ref, mine_ref, other_ref, refs[-1])
    odd = lax.rem(lax.axis_index("tile"), 2) == 1
    pl.when(jnp.logical_not(odd))(lambda: run(1 - which))
    pl.when(odd)(lambda: run(which))


def border_rows(vector_ref, border_ref, mine_ref, other_ref, out_ref, side):
    _, _, rows, cells = other_ref.shape
    start, near = side * (rows - EDGE), side * (8 - EDGE)
    total_rows = out_ref.shape[0]
    per_tile = total_rows // (cells // LANES)
    valid = [vector_ref[slot, 0:1, :] > 0.5 for slot in range(SLOTS)]
    sublane = lax.broadcasted_iota(jnp.int32, (8, LANES), 0)
    phase = [lax.rem(sublane + shift, EDGE) for shift in range(EDGE)]
    is_zero = [value == 0 for value in phase]
    is_one = [value == 1 for value in phase]
    whole = {}
    for t in range(cells // LANES):
        for slot in range(SLOTS):
            lines = []
            for i in range(EDGE):
                here = mine_ref[side, slot, near + i : near + i + 1, lanes_of(t)]
                there = other_ref[0, slot, start + i : start + i + 1, lanes_of(t)]
                lines.append(jnp.broadcast_to(jnp.where(valid[slot], here, there), (8, LANES)))
            for shift in range(EDGE):
                whole[t, slot, shift] = jnp.where(
                    is_zero[shift], lines[0], jnp.where(is_one[shift], lines[1], lines[2])
                )
        for row in range(0, total_rows, 8):
            if (row + 7) // per_tile != t:
                continue
            total = None
            for slot in range(SLOTS):
                field = whole[t, slot, row % EDGE]
                if row // per_tile != t:
                    field = jnp.where(sublane < per_tile * t - row, whole[t - 1, slot, row % EDGE], field)
                term = border_ref[slot, side, row : row + 8, :] * field
                total = term if total is None else total + term
            out_ref[row : row + 8, :] = total


def bulk_kernel(
    owner_ref, taps_x_ref, taps_y_ref, matrix, matrix_t, perturb_ref, other_ref, pair_ref, next_ref,
    mine_hbm, control_hbm, velocity_hbm,
    local_ref, cross_pair_ref, cross_next_ref, square_ref, control_ref, velocity_ref,
    mine, field, rows_of, packed, left, result, sems,
):
    members, _, rows, cells = perturb_ref.shape
    count = cells // LANES
    here = EDGE * members
    mine_copy = pltpu.make_async_copy(mine_hbm, mine, sems.at[2])
    mine_copy.start()
    control_copy = pltpu.make_async_copy(control_hbm, control_ref, sems.at[0])
    velocity_copy = pltpu.make_async_copy(velocity_hbm, velocity_ref, sems.at[1])
    control_copy.start()
    velocity_copy.start()
    me = lax.axis_index("member")
    tile = lax.axis_index("tile")
    tiles = lax.axis_size("tile")
    taps_x = [taps_x_ref[k] for k in range(7)]
    taps_y = [taps_y_ref[k] for k in range(7)]
    first_taps, last_taps = taps_x[0:EDGE], taps_x[6 : 6 - EDGE : -1]
    for half in range(2):
        rows_of[half, :, 0:8, :] = jnp.zeros((count, 8, LANES), F32)
        rows_of[half, :, rows + 8 : rows + 16, :] = jnp.zeros((count, 8, LANES), F32)
    clear_packed(packed, count)

    def unpack(up_ref, down_ref):
        for t in range(count):
            packed[0, t, 0:here, :] = up_ref[here * t : here * (t + 1), :]
            packed[1, t, 8 : 8 + here, :] = down_ref[here * t : here * (t + 1), :]

    by_parity(unpack, pair_ref, next_ref)
    border_levels(packed, count, first_taps, last_taps, taps_y, left, matrix[...], result)
    weights = [jnp.where(tile < tiles - 1, 1.0, 0.0).astype(F32), jnp.where(tile > 0, 1.0, 0.0).astype(F32)]
    squares = jnp.zeros((8, LANES), F32)
    for side in range(2):
        total = [jnp.zeros((8, LANES), F32) for _ in range(4)]
        for t in range(count):
            for step in range(4):
                value = result[64 * t + 32 * side + 8 * step : 64 * t + 32 * side + 8 * step + 8, :]
                total[step] += value * value
        squares += weights[side] * ((total[0] + total[1]) + (total[2] + total[3]))

    mine_copy.wait()
    for slot in range(SLOTS):
        field[slot] = jnp.where(owner_ref[slot] == me, mine[0, slot], other_ref[0, slot])

    def pair_step(pair, carry):
        for half in range(2):
            member = 2 * pair + half
            for t in range(count):
                product = perturb_ref[member, 0, :, lanes_of(t)].astype(F32) * field[0, :, lanes_of(t)]
                for slot in range(1, SLOTS):
                    product += perturb_ref[member, slot, :, lanes_of(t)].astype(F32) * field[slot, :, lanes_of(t)]
                rows_of[half, t, 8 : 8 + rows, :] = product
        blocks = []
        size = 2 * rows
        for half in range(2):
            for row in range(0, rows, 8):
                block = []
                for t in range(count):
                    total = None
                    for k in range(7):
                        term = taps_x[k] * rows_of[half, t, row + k + 5 : row + k + 13, :]
                        total = term if total is None else total + term
                    block.append(total)
                blocks.append(columns(block, taps_y))
                if len(blocks) == 2:
                    store_split(left, size, half * rows + row - 8, *blocks)
                    blocks = []
        pl.when(pair == 0)(control_copy.wait)
        group = 4
        for first in range(0, count, group):
            out = mixed(left, size * first, size * group, matrix[...])
            for t in range(first, first + group):
                for half in range(2):
                    member = 2 * pair + half
                    base = size * (t - first) + rows * half
                    value = control_ref[member, :, lanes_of(t)] + out[base : base + rows]
                    local_ref[member, :, lanes_of(t)] = value
                    squared = value * value
                    for row in range(0, rows, 8):
                        carry += squared[row : row + 8]
                    packed[0, t, pl.ds(EDGE * member, EDGE), :] = value[rows - EDGE : rows]
                    packed[1, t, pl.ds(8 + EDGE * member, EDGE), :] = value[0:EDGE]
        return carry

    square_ref[...] = lax.fori_loop(0, members // 2, pair_step, squares)
    velocity_copy.wait()
    border_levels(packed, count, last_taps, first_taps, taps_y[::-1], left, matrix_t[...], result)

    def pack(cross_down_ref, cross_up_ref):
        for t in range(count):
            cross_down_ref[here * t : here * (t + 1), :] = result[64 * t : 64 * t + here, :]
            cross_up_ref[here * t : here * (t + 1), :] = result[64 * t + 32 : 64 * t + 32 + here, :]

    by_parity(pack, cross_pair_ref, cross_next_ref)


def cross_kernel(square_ref, cross_pair_ref, cross_next_ref, from_pair_ref, from_next_ref, total_ref):
    total = [jnp.zeros((8, LANES), F32) for _ in range(4)]
    for step, row in enumerate(range(0, cross_pair_ref.shape[0], 8)):
        at = slice(row, row + 8)
        which = 2 * (step % 2)
        total[which] += cross_pair_ref[at] * from_pair_ref[at]
        total[which + 1] += cross_next_ref[at] * from_next_ref[at]
    whole = square_ref[...] + 2.0 * ((total[0] + total[1]) + (total[2] + total[3]))
    total_ref[...] = jnp.sum(whole, axis=0, keepdims=True)


def correct_kernel(
    vector_ref, matrix, from_pair_ref, from_next_ref, local_ref, gradient_ref, packed, left, result
):
    members, rows, cells = local_ref.shape
    count = cells // LANES
    here = EDGE * members
    taps_x = [vector_ref[SLOTS + k] for k in range(7)]
    taps_y = [vector_ref[SLOTS + 7 + k] for k in range(7)]
    clear_packed(packed, count)

    def unpack(from_right_ref, from_left_ref):
        for t in range(count):
            packed[0, t, 0:here, :] = from_left_ref[here * t : here * (t + 1), :]
            packed[1, t, 8 : 8 + here, :] = from_right_ref[here * t : here * (t + 1), :]

    by_parity(unpack, from_pair_ref, from_next_ref)
    border_levels(
        packed, count, taps_x[0:EDGE], taps_x[6 : 6 - EDGE : -1], taps_y, left, matrix[...], result
    )
    for member in range(members):
        for t in range(count):
            at = 64 * t + EDGE * member
            gradient_ref[member, 0:EDGE, lanes_of(t)] += result[at : at + EDGE, :]
            gradient_ref[member, rows - EDGE : rows, lanes_of(t)] += result[at + 32 : at + 32 + EDGE, :]


def update_kernel(
    entries, near_ref, far_ref, control_ref, velocity_ref, gradient_ref,
    new_control_hbm, new_velocity_hbm, new_control, new_velocity, sems,
):
    members, rows, cells = control_ref.shape
    mean = jnp.sum(near_ref[...] + far_ref[...], keepdims=True) / entries
    scale = lax.rsqrt(mean + 1e-06)
    copies = []
    for member in range(members):
        for start in range(0, rows, 8):
            tile = slice(start, start + 8)
            moved = 0.9 * velocity_ref[member, tile] + scale * gradient_ref[member, tile]
            new_velocity[member, tile] = moved
            new_control[member, tile] = control_ref[member, tile] - 0.5 * moved
        for which, (src, dst) in enumerate(((new_control, new_control_hbm), (new_velocity, new_velocity_hbm))):
            copy = pltpu.make_async_copy(src.at[member], dst.at[member], sems.at[which, member])
            copy.start()
            copies.append(copy)
    for copy in copies:
        copy.wait()


def body(control, velocity, perturb, adjoint_forcing, slot_owner, taps_x, taps_y, vertical_mix):
    members, rows, cells = control.shape
    count = cells // LANES
    tiles = lax.axis_size("tile")
    groups = lax.axis_size("member")
    owner = slot_owner.reshape(SLOTS)
    swap = [(0, 1), (1, 0)]
    other = lax.ppermute(adjoint_forcing, "member", swap)
    edges = EDGE * members * count
    square_matrix = (2 * LANES, 2 * LANES)
    perturb, mine, border, matrix, matrix_t, vectors = pl.pallas_call(
        stage_kernel,
        name="stage",
        out_shape=(
            jax.ShapeDtypeStruct(perturb.shape, perturb.dtype),
            jax.ShapeDtypeStruct((2, SLOTS, 8, cells), F32),
            jax.ShapeDtypeStruct((SLOTS, 2, edges, LANES), F32),
            jax.ShapeDtypeStruct(square_matrix, BF16),
            jax.ShapeDtypeStruct(square_matrix, BF16),
            jax.ShapeDtypeStruct((SLOTS + 14, 8, LANES), F32),
        ),
        in_specs=[HBM] * 6,
        out_specs=(VMEM,) * 6,
        scratch_shapes=[
            pltpu.VMEM(vertical_mix.shape, F32),
            pltpu.SMEM((SLOTS,), jnp.int32),
            pltpu.SMEM((7,), F32),
            pltpu.SMEM((7,), F32),
            pltpu.SemaphoreType.DMA((members + 6,)),
        ],
        compiler_params=params(8),
        cost_estimate=cost(0, 8_000_000),
    )(*map(in_hbm, (perturb, adjoint_forcing, vertical_mix, owner, taps_x, taps_y)))
    packed = jax.ShapeDtypeStruct((edges, LANES), F32)
    sent = []
    for which in range(2):
        sent.append(
            pl.pallas_call(
                functools.partial(border_kernel, which),
                name=f"border_product_{which}",
                out_shape=packed,
                in_specs=[VMEM, VMEM, VMEM, VMEM] + [pl.BlockSpec(memory_space=pl.ANY)] * which,
                out_specs=VMEM,
                compiler_params=params(8),
                cost_estimate=cost(2_000_000, 2_000_000),
            )(vectors, border, mine, other, *sent)
        )
    pair, after = sent
    swaps = [(i, i + 1) for i in range(tiles - 1)] + [(i + 1, i) for i in range(tiles - 1)]
    from_next = lax.ppermute(after, "tile", [(i, j) for i, j in swaps if min(i, j) % 2 == 1])
    from_pair = lax.ppermute(pair, "tile", [(i, j) for i, j in swaps if min(i, j) % 2 == 0])
    border_scratch = [
        pltpu.VMEM((2, count, 40, LANES), F32),
        pltpu.VMEM((count * 64, 2 * LANES), BF16),
        pltpu.VMEM((count * 64, LANES), F32),
    ]
    whole = jax.ShapeDtypeStruct(control.shape, F32)
    local, cross_pair, cross_next, square, control, velocity = pl.pallas_call(
        bulk_kernel,
        name="bulk",
        out_shape=(whole, packed, packed, jax.ShapeDtypeStruct((8, LANES), F32), whole, whole),
        in_specs=[SMEM, SMEM, SMEM] + [VMEM] * 6 + [HBM, HBM, HBM],
        out_specs=(VMEM,) * 6,
        scratch_shapes=[
            pltpu.VMEM(adjoint_forcing.shape, F32),
            pltpu.VMEM((SLOTS, rows, cells), F32),
            pltpu.VMEM((2, count, rows + 16, LANES), F32),
            *border_scratch,
            pltpu.SemaphoreType.DMA((3,)),
        ],
        compiler_params=params(24),
        cost_estimate=cost(9_000_000_000, 12_000_000),
    )(
        owner, taps_x, taps_y, matrix, matrix_t, perturb, other, pair, after,
        in_hbm(adjoint_forcing), in_hbm(control), in_hbm(velocity),
    )
    near = pl.pallas_call(
        cross_kernel,
        name="cross_term",
        out_shape=jax.ShapeDtypeStruct((1, LANES), F32),
        in_specs=[VMEM] * 5,
        out_specs=VMEM,
        compiler_params=params(8),
        cost_estimate=cost(200_000, 1_000_000),
    )(square, cross_pair, cross_next, from_pair, from_next)
    gradient = pl.pallas_call(
        correct_kernel,
        name="border_correction",
        out_shape=whole,
        in_specs=[VMEM] * 5,
        out_specs=VMEM,
        scratch_shapes=border_scratch,
        input_output_aliases={4: 0},
        compiler_params=params(16),
        cost_estimate=cost(2_000_000_000, 2_000_000),
    )(vectors, matrix, from_pair, from_next, local)
    near = near + lax.ppermute(near, "member", swap)
    steps = []
    width = 1
    while width < tiles:
        steps.append([(groups * i + g, groups * (i ^ width) + groups - 1 - g) for i in range(tiles) for g in range(groups)])
        width *= 2
    for pairs in steps[:-1]:
        near = near + lax.ppermute(near, ("tile", "member"), pairs)
    far = lax.ppermute(near, ("tile", "member"), steps[-1])
    entries = members * groups * rows * tiles * cells
    return tuple(
        pl.pallas_call(
            functools.partial(update_kernel, float(entries)),
            name="update",
            out_shape=(whole, whole),
            in_specs=[VMEM] * 5,
            out_specs=(HBM, HBM),
            scratch_shapes=[
                pltpu.VMEM(control.shape, F32),
                pltpu.VMEM(control.shape, F32),
                pltpu.SemaphoreType.DMA((2, members)),
            ],
            compiler_params=params(16),
            cost_estimate=cost(3_000_000, 12_000_000),
        )(near, far, control, velocity, gradient)
    )


def solution(mesh):
    placed = (
        P(("window", "member"), "tile", None),
        P(("window", "member"), "tile", None),
        P(("window", "member"), None, "tile", None),
        P(("window", "member"), None, "tile", None),
        P("window", "tile"),
        P(),
        P(),
        P(),
    )
    return jax.shard_map(
        body,
        mesh=mesh,
        in_specs=placed,
        out_specs=(P(("window", "member"), "tile", None), P(("window", "member"), "tile", None)),
        check_vma=False,
    )
```
